256 devices in a mesh: pb: 32 (over z_lo, y, x), wa: 8 (over z_hi, core).
Axes of the slice: x: 4, y: 4, z: 8 (z_hi: 4, z_lo: 2; z = z_hi * 2 + z_lo), core: 2. Of those that a mesh axis runs over, the one named last changes fastest.
Arguments:
- propagator: bfloat16 [80, 4096], P(None, 'pb'), may hold values from -6 to 6
- vertex: bfloat16 [256, 16, 57600], P('pb', 'wa'), may hold values from -0.005859375 to 0.005859375
- momentum_shift: int32 [256, 4096], P('pb'), may hold values from 0 to 4095, as said below
- frequency_shift: int32 [16, 48], P('wa'), may hold values from 0 to 79, as said below
Outputs:
- flow: float32 [48, 4096], P('wa', 'pb')
The draws below stay inside these ranges and needn't reach their ends.
Inputs may be any that keep to these rules, and one draw needn't show every extreme that they name: momentum_shift[q, k] is x * 64 + y for the lattice momentum k shifted by the q-th transfer momentum of the window, periodic on the 64 x 64 lattice; every row is a permutation, and the 256 transfer momenta are distinct. frequency_shift[w, m] = m + o_w, where the bosonic offsets o_w are distinct, increasing in w, with o_0 = 0 and the last one 32.
All inputs are finite; a program needn't handle non-finite values.
Results may differ from the reference program's by a relative error of at most 0.0025.
Values may be sent and summed in bfloat16 or wider, within the bound.
A program may use at most 64 MiB of HBM per device.

```python
import math
import jax
import jax.numpy as jnp
from jax import lax

LAT = 64
NK = 4096
NFF = 5
NF = 48
NB = 240
Q = 256
W = 16
OMAX = 32
NS = 80


def draw_momentum_shift(key, part):
    key = jax.random.fold_in(key, 11)
    chosen = jax.random.permutation(key, jnp.arange(NK, dtype=jnp.int32))[:Q]
    shift_x = (chosen // LAT)[:, None]
    shift_y = (chosen % LAT)[:, None]
    momenta = jnp.arange(NK, dtype=jnp.int32)
    coord_x = momenta // LAT
    coord_y = momenta % LAT
    moved_x = (coord_x[None, :] + shift_x) % LAT
    moved_y = (coord_y[None, :] + shift_y) % LAT
    return (moved_x * LAT + moved_y).astype(jnp.int32)


def draw_frequency_shift(key, part):
    key = jax.random.fold_in(key, 23)
    inner = jax.random.permutation(key, jnp.arange(1, OMAX, dtype=jnp.int32))[:W - 2]
    offsets = jnp.concatenate([jnp.zeros((1,), jnp.int32), inner, jnp.full((1,), OMAX, jnp.int32)])
    offsets = jnp.sort(offsets)
    return (offsets[:, None] + jnp.arange(NF, dtype=jnp.int32)[None, :]).astype(jnp.int32)


def shard_levels(key, shape, pieces, low, top_value):
    loudness = 1.0
    for dim, parts in pieces:
        steps = jax.random.uniform(jax.random.fold_in(jax.random.fold_in(key, 6), dim), (parts,), jnp.float32, low / len(pieces), top_value / len(pieces))
        loudness = loudness * jnp.repeat(jnp.exp(steps), shape[dim] // parts).reshape((-1,) + (1,) * (len(shape) - 1 - dim))
    return loudness


def normal_values(own_key, dims, spread, limit, shards=(), kind=jnp.bfloat16):
    level = shard_levels(own_key, dims, shards, -0.22, 0.18) if shards else 1.0
    result = jax.random.normal(own_key, dims, jnp.float32) * spread * level
    return jnp.minimum(jnp.maximum(result, -limit), limit).astype(kind)


def setup_inputs(seed: int = 0) -> dict:
    key_list = jax.random.split(jax.random.key(seed), 5)
    propagator = normal_values(key_list[0], (NS, NK), 1.0, 6.0, ((1, 32),))
    vertex = normal_values(key_list[1], (Q, W, NB * NB), (NB * Q * W) ** -0.5, 0.005859375, ((0, 32), (1, 8)))
    momentum_shift = draw_momentum_shift(jax.random.fold_in(key_list[4], 71), 0)
    frequency_shift = draw_frequency_shift(jax.random.fold_in(key_list[4], 71), 0)
    return dict(propagator=propagator, vertex=vertex, momentum_shift=momentum_shift, frequency_shift=frequency_shift)


def form_factors(momenta):
    angle_x = (momenta // LAT).astype(jnp.float32) * (2.0 * math.pi / LAT)
    angle_y = (momenta % LAT).astype(jnp.float32) * (2.0 * math.pi / LAT)
    root_two = math.sqrt(2.0)
    return jnp.stack([jnp.ones_like(angle_x), root_two * jnp.cos(angle_x), root_two * jnp.cos(angle_y), root_two * jnp.sin(angle_x), root_two * jnp.sin(angle_y)])

def pair_flow(propagator, block, shift_row, frequency_row, factors):
    selected = jnp.take(propagator, frequency_row, axis=0)
    shifted = jnp.take(selected, shift_row, axis=1).astype(jnp.float32)
    projected = (factors[:, None, :] * shifted[None, :, :]).reshape(NFF * NF, -1).astype(jnp.bfloat16)
    contracted = jnp.dot(block.reshape(NB, NB), projected, preferred_element_type=jnp.float32)
    return lax.optimization_barrier(jnp.sum(factors[:, None, :] * contracted.reshape(NFF, NF, -1), axis=0))

def reference(propagator, vertex, momentum_shift, frequency_shift):
    factors = form_factors(jnp.arange(NK, dtype=jnp.int32))

    def accumulate(total, pair_index):
        q_index = pair_index // W
        w_index = pair_index % W
        term = pair_flow(propagator, vertex[q_index, w_index], momentum_shift[q_index], frequency_shift[w_index], factors)
        return (total + term, None)
    total, unused = lax.scan(accumulate, jnp.zeros((NF, NK), jnp.float32), jnp.arange(Q * W, dtype=jnp.int32))
    return -total
```

```python
import math

import jax
import jax.numpy as jnp
import numpy as np
from jax import lax
from jax.experimental import pallas as pl
from jax.experimental.pallas import tpu as pltpu

LAT = 64
F32 = jnp.float32
BF16 = jnp.bfloat16
I32 = jnp.int32
NQ = 8
NB = 13
ROWS = 320
KQ = 128
STEPS = 16

BLOCKS = (
    ((0, 0, 1), (1, 1, 1), (2, 2, 1), (3, 3, 1), (4, 4, 1)),
    ((0, 1, 1), (1, 0, 1)),
    ((0, 2, 1), (2, 0, 1)),
    ((0, 3, 1), (3, 0, 1)),
    ((0, 4, 1), (4, 0, 1)),
    ((1, 1, 1), (3, 3, -1)),
    ((1, 3, 1), (3, 1, 1)),
    ((2, 2, 1), (4, 4, -1)),
    ((2, 4, 1), (4, 2, 1)),
    ((1, 2, 1), (2, 1, 1)),
    ((1, 4, 1), (4, 1, 1)),
    ((2, 3, 1), (3, 2, 1)),
    ((3, 4, 1), (4, 3, 1)),
)


def minus_functions():
    k = np.arange(LAT * LAT)
    a = (k // LAT) * (2.0 * math.pi / LAT)
    b = (k % LAT) * (2.0 * math.pi / LAT)
    root = math.sqrt(2.0)
    ca, cb, sa, sb = np.cos(a), np.cos(b), np.sin(a), np.sin(b)
    rows = [
        np.ones_like(a),
        root * ca,
        root * cb,
        root * sa,
        root * sb,
        np.cos(2 * a),
        np.sin(2 * a),
        np.cos(2 * b),
        np.sin(2 * b),
        2 * ca * cb,
        2 * ca * sb,
        2 * cb * sa,
        2 * sa * sb,
    ]
    table = np.zeros((16, LAT * LAT), np.float32)
    table[:NB] = -np.stack(rows)
    return np.ascontiguousarray(table.reshape(16, 32, 128).transpose(1, 0, 2))


def kernel(
    prop, vert, mom, freq, table, out,
    vb, s32, wown, wrecv, lhs, gs, dup, rhs0, rhs1, tab, momv, freqv,
    ssend, srecv, red, fsend, frecv, whole,
    in_sem, v_sem, ag_s, ag_r, z_s, z_r, c_s, c_r, c2_s, c2_r, w_s, w_r, s_s, s_r, f_s, f_r,
):
    p = lax.axis_index("pb")
    wa = lax.axis_index("wa")
    zl = p // 16
    yy = (p // 4) % 4
    xx = p % 4
    core = wa % 2
    z = (wa // 2) * 2 + zl

    def plane(e, sign):
        ey = e // 4
        ex = e % 4
        return ((yy + sign * ey + 4) % 4) * 4 + (xx + sign * ex + 4) % 4

    def column(dz, dc):
        zz = (z + dz) % 8
        return ((zz % 2) * 16 + p % 16, (zz // 2) * 2 + (core + dc) % 2)

    def remote(src, dst, send, recv, device):
        return pltpu.make_async_remote_copy(
            src_ref=src, dst_ref=dst, send_sem=send, recv_sem=recv,
            device_id=device, device_id_type=pl.DeviceIdType.MESH,
        )

    def each(n, body):
        def step(i, carry):
            body(i)
            return carry

        lax.fori_loop(0, n, step, 0)

    c_mom = pltpu.make_async_copy(mom.at[:, pl.ds(0, 128)], momv, in_sem.at[0])
    c_freq = pltpu.make_async_copy(freq, freqv, in_sem.at[1])
    c_tab = pltpu.make_async_copy(table, tab, in_sem.at[2])
    c_own = pltpu.make_async_copy(prop, gs.at[p], in_sem.at[3])
    c_mom.start()
    c_freq.start()

    def piece(i):
        rows = pl.ds(pl.multiple_of(i * 800, 800), 800)
        return pltpu.make_async_copy(vert.at[rows], vb.at[rows], v_sem.at[i])

    each(9, lambda i: piece(i).start())
    c_own.start()
    c_tab.start()

    barrier = pltpu.get_barrier_semaphore()

    def greet(i):
        e = i + 1
        pl.semaphore_signal(
            barrier, inc=1, device_id=(zl * 16 + plane(e, 1), wa), device_id_type=pl.DeviceIdType.MESH
        )
        pl.semaphore_signal(
            barrier, inc=1, device_id=column(e // 2, e % 2), device_id_type=pl.DeviceIdType.MESH
        )

    each(15, greet)

    def widen(i):
        piece(i).wait()
        for t in range(5):
            rows = pl.ds(pl.multiple_of(i * 800 + t * 160, 160), 160)
            s32[rows, :] = vb[rows, :].astype(F32)

    each(9, widen)
    s32[pl.ds(7200, 64), :] = jnp.zeros((64, 128), F32)

    def clear(q):
        for half in range(2):
            wown[half, q, pl.ds(312, 8), :] = jnp.zeros((8, 128), F32)
        for r in (rhs0, rhs1):
            r[pl.ds(pl.multiple_of(q * KQ + 80, 16), KQ - 80), :] = jnp.zeros((KQ - 80, 256), BF16)

    each(NQ, clear)
    c_mom.wait()
    c_freq.wait()
    pl.semaphore_wait(barrier, 30)

    def item(i):
        return 2 * i + core

    def ag(i):
        e = item(i)
        return remote(prop, gs.at[p], ag_s.at[i], ag_r.at[i], (zl * 16 + plane(e, 1), wa))

    up = 1 + 6 * core

    def own_slot(i):
        return zl * 16 + plane(item(i), -1)

    def far_slot(i):
        return (1 - zl) * 16 + plane(item(i), -1)

    def zf(i):
        slot = own_slot(i)
        return remote(gs.at[slot], gs.at[slot], z_s.at[i], z_r.at[i], column(up, 0))

    def cf(i):
        slot = own_slot(i)
        return remote(gs.at[slot], gs.at[slot], c_s.at[i], c_r.at[i], column(0, 1))

    def cf2(i):
        slot = far_slot(i)
        return remote(gs.at[slot], gs.at[slot], c2_s.at[i], c2_r.at[i], column(0, 1))

    def start_ag(i):
        @pl.when(item(i) != 0)
        def _():
            ag(i).start()

    each(8, start_ag)
    c_own.wait()

    def pass_on(i):
        @pl.when(item(i) != 0)
        def _():
            ag(i).wait_recv()
            cf(i).start()

        zf(i).start()

    def pass_on_far(i):
        zf(i).wait_recv()
        cf2(i).start()

    lane = lax.broadcasted_iota(I32, (8, 128), 1)

    def w_send(q):
        return remote(wown.at[1 - core, q], wrecv.at[q], w_s.at[q], w_r.at[q], column(0, 1))

    def prepare(q):
        shifts = [freqv[w, 0] for w in range(2)]
        valid = [(lane >= o) & (lane < o + 48) for o in shifts]
        for i in range(8):
            total = [None] * NB
            for w in range(2):
                blocks = {}
                for n2 in range(5):
                    off = 240 * i + 48 * n2
                    s, start = off // 128, off % 128
                    amount = (shifts[w] + (128 - start)) % 128
                    for n in range(5):
                        row = q * 900 + 180 * n + w + 2 * s
                        value = s32[pl.ds(row, 8, stride=30), :]
                        if start > 80:
                            after = s32[pl.ds(row + 2, 8, stride=30), :]
                            value = jnp.where(lane < start, after, value)
                        blocks[n, n2] = pltpu.roll(value, amount, 1)
                for f in range(NB):
                    term = None
                    for n, n2, sign in BLOCKS[f]:
                        if term is None:
                            term = blocks[n, n2]
                        elif sign > 0:
                            term = term + blocks[n, n2]
                        else:
                            term = term - blocks[n, n2]
                    term = jnp.where(valid[w], term, 0.0)
                    total[f] = term if total[f] is None else total[f] + term
            for f in range(NB):
                wown[i // 4, q, pl.ds(24 * f + 6 * (i % 4), 6), :] = total[f][0:6]
        w_send(q).start()
        pass_on(q)

    each(NQ, prepare)
    each(8, pass_on_far)

    def settle(i):
        e = 2 * i + (1 - core)
        near = zl * 16 + plane(e, -1)
        far = (1 - zl) * 16 + plane(e, -1)

        @pl.when(e != 0)
        def _():
            remote(gs.at[near], gs.at[near], c_s.at[i], c_r.at[i], column(0, 1)).wait_recv()

        remote(gs.at[far], gs.at[far], c2_s.at[i], c2_r.at[i], column(0, 1)).wait_recv()

    each(8, settle)

    low = lax.broadcasted_iota(I32, (80, 128), 1) < 64

    def double(b):
        value = gs[b]
        turned = pltpu.roll(value, 64, 1)
        dup[2 * b] = jnp.where(low, value, turned)
        dup[2 * b + 1] = jnp.where(low, turned, value)

    each(32, double)

    for q in range(NQ):
        w_send(q).wait_recv()
        lhs[:, KQ * q : KQ * (q + 1)] = (wown[core, q] + wrecv[q]).astype(BF16)
    c_tab.wait()

    def build(step, ref):
        block = plane(15 - step, 1)
        for q in range(NQ):
            shift = momv[q, 0]
            qx = shift // 64
            amount = (128 - shift % 64) % 128
            for half in range(2):
                x = 2 * (block + 16 * half) + qx
                first = pltpu.roll(dup[x % 64], amount, 1)
                second = pltpu.roll(dup[(x + 1) % 64], amount, 1)
                ref[KQ * q : KQ * q + 80, 128 * half : 128 * half + 128] = jnp.where(low, first, second)

    def s_copy(e):
        return remote(ssend.at[e], srecv.at[e], s_s.at[e], s_r.at[e], (zl * 16 + plane(e, 1), wa))

    def contract(step, ref):
        e = 15 - step
        block = plane(e, 1)
        acc = jnp.dot(lhs[...], ref[...], preferred_element_type=F32)
        for half in range(2):
            factors = tab[block + 16 * half]
            flow = None
            for f in range(NB):
                term = factors[f : f + 1, :] * acc[24 * f : 24 * f + 24, 128 * half : 128 * half + 128]
                flow = term if flow is None else flow + term
            ssend[e, half] = flow

        @pl.when(e != 0)
        def _():
            s_copy(e).start()

    build(0, rhs0)

    def two(i):
        build(2 * i + 1, rhs1)
        contract(2 * i, rhs0)
        build((2 * i + 2) % STEPS, rhs0)
        contract(2 * i + 1, rhs1)

    each(STEPS // 2, two)

    red[...] = ssend[0]

    def gather_sum(i):
        e = 15 - i
        s_copy(e).wait_recv()
        red[...] += srecv[e]

    each(15, gather_sum)

    for zt in range(2):
        for h in range(4):
            first = 3 * (h // 2) + h % 2
            for a in range(2):
                fsend[zt * 4 + h, 4 * a : 4 * a + 4, :] = red[zt, pl.ds(first + a, 4, stride=6), :]

    def f_copy(d):
        zz = (z + d // 2) % 8
        return remote(
            fsend.at[(zz % 2) * 4 + zz // 2], frecv.at[d], f_s.at[d], f_r.at[d], column(d // 2, d % 2)
        )

    each(15, lambda i: f_copy(15 - i).start())
    same = fsend[zl * 4 + z // 2]
    other = jnp.zeros((8, 128), F32)
    for d in range(15, 0, -1):
        f_copy(d).wait_recv()
        if d % 2 == 0:
            same = same + frecv[d]
        else:
            other = other + frecv[d]
    zero = core == 0
    one = jnp.where(zero, same, other)
    two_ = jnp.where(zero, other, same)
    whole[0:4, :] = one[0:4]
    whole[4:8, :] = two_[0:4]
    whole[8:12, :] = one[4:8]
    whole[12:16, :] = two_[4:8]
    out[...] = whole[pl.ds(6 * core + 4 * ((z // 2) % 2), 6), :]

    def drain(i):
        @pl.when(item(i) != 0)
        def _():
            ag(i).wait_send()
            cf(i).wait_send()

        zf(i).wait_send()
        cf2(i).wait_send()
        w_send(i).wait_send()

    each(8, drain)

    def drain_sums(i):
        s_copy(i + 1).wait_send()
        f_copy(i + 1).wait_send()

    each(15, drain_sums)


def local(propagator, vertex, momentum_shift, frequency_shift):
    rows = vertex.transpose(0, 2, 1).reshape(3600, 128, 2).transpose(0, 2, 1).reshape(7200, 128)
    dma = pltpu.SemaphoreType.DMA
    vmem = pltpu.VMEM
    scratch = [
        vmem((7200, 128), BF16),
        vmem((7264, 128), F32),
        vmem((2, NQ, ROWS, 128), F32),
        vmem((NQ, ROWS, 128), F32),
        vmem((ROWS, NQ * KQ), BF16),
        vmem((32, 80, 128), BF16),
        vmem((64, 80, 128), BF16),
        vmem((NQ * KQ, 256), BF16),
        vmem((NQ * KQ, 256), BF16),
        vmem((32, 16, 128), F32),
        pltpu.SMEM((8, 128), I32),
        pltpu.SMEM((2, 48), I32),
        vmem((16, 2, 24, 128), F32),
        vmem((16, 2, 24, 128), F32),
        vmem((2, 24, 128), F32),
        vmem((8, 8, 128), F32),
        vmem((16, 8, 128), F32),
        vmem((16, 128), F32),
        dma((4,)),
        dma((9,)),
    ]
    scratch += [dma((8,))] * 10 + [dma((16,))] * 4
    return pl.pallas_call(
        kernel,
        out_shape=jax.ShapeDtypeStruct((6, 128), F32),
        in_specs=[pl.BlockSpec(memory_space=pl.ANY)] * 5,
        out_specs=pl.BlockSpec(memory_space=pltpu.VMEM),
        scratch_shapes=scratch,
        compiler_params=pltpu.CompilerParams(
            collective_id=0, has_side_effects=True, vmem_limit_bytes=48 * 1024 * 1024
        ),
    )(propagator, rows, momentum_shift, frequency_shift, jnp.asarray(minus_functions()))


def solution(mesh):
    from jax.sharding import PartitionSpec as P

    in_specs = (P(None, "pb"), P("pb", "wa", None), P("pb", None), P("wa", None))
    out_specs = P("wa", "pb")
    return jax.shard_map(local, mesh=mesh, in_specs=in_specs, out_specs=out_specs, check_vma=False)
```

```python
import math

import jax
import jax.numpy as jnp
import numpy as np
from jax import lax
from jax.experimental import pallas as pl
from jax.experimental.pallas import tpu as pltpu

LAT = 64
F32 = jnp.float32
BF16 = jnp.bfloat16
I32 = jnp.int32
NQ = 8
NB = 13
ROWS = NB * 48
KQ = 80
DIST = (0, 1, 2, 1)

OFFSETS = sorted(
    ((a, y, x) for a in range(2) for y in range(4) for x in range(4) if a + y + x),
    key=lambda o: -(o[0] + DIST[o[1]] + DIST[o[2]]),
)
EVEN = [o for o in OFFSETS if sum(o) % 2 == 0]
ODD = [o for o in OFFSETS if sum(o) % 2 == 1]

BLOCKS = (
    ((0, 0, 1), (1, 1, 1), (2, 2, 1), (3, 3, 1), (4, 4, 1)),
    ((0, 1, 1), (1, 0, 1)),
    ((0, 2, 1), (2, 0, 1)),
    ((0, 3, 1), (3, 0, 1)),
    ((0, 4, 1), (4, 0, 1)),
    ((1, 1, 1), (3, 3, -1)),
    ((1, 3, 1), (3, 1, 1)),
    ((2, 2, 1), (4, 4, -1)),
    ((2, 4, 1), (4, 2, 1)),
    ((1, 2, 1), (2, 1, 1)),
    ((1, 4, 1), (4, 1, 1)),
    ((2, 3, 1), (3, 2, 1)),
    ((3, 4, 1), (4, 3, 1)),
)


def minus_functions():
    k = np.arange(LAT * LAT)
    a = (k // LAT) * (2.0 * math.pi / LAT)
    b = (k % LAT) * (2.0 * math.pi / LAT)
    root = math.sqrt(2.0)
    ca, cb, sa, sb = np.cos(a), np.cos(b), np.sin(a), np.sin(b)
    rows = [
        np.ones_like(a),
        root * ca,
        root * cb,
        root * sa,
        root * sb,
        np.cos(2 * a),
        np.sin(2 * a),
        np.cos(2 * b),
        np.sin(2 * b),
        2 * ca * cb,
        2 * ca * sb,
        2 * cb * sa,
        2 * sa * sb,
    ]
    table = np.zeros((16, LAT * LAT), np.float32)
    table[:NB] = -np.stack(rows)
    return np.ascontiguousarray(table.reshape(16, 32, 128).transpose(1, 0, 2))


def kernel(
    prop, vert, mom, freq, table, out,
    vb, s32, wown, wrecv, lhs, gs, dup, rhs0, rhs1, tab, momv, freqv,
    ssend, srecv, red, fsend, frecv,
    in_sem, v_sem, w_s, w_r, f_s, f_r, ag_s, ag_r, c_s, c_r, s_s, s_r,
):
    p = lax.axis_index("pb")
    wa = lax.axis_index("wa")
    zl = p // 16
    yy = (p // 4) % 4
    xx = p % 4
    core = wa % 2
    z = (wa // 2) * 2 + zl
    other = 1 - core
    sibling = (p, (wa // 2) * 2 + other)

    def remote(src, dst, send, recv, device):
        return pltpu.make_async_remote_copy(
            src_ref=src, dst_ref=dst, send_sem=send, recv_sem=recv,
            device_id=device, device_id_type=pl.DeviceIdType.MESH,
        )

    def signal(device):
        pl.semaphore_signal(barrier, inc=1, device_id=device, device_id_type=pl.DeviceIdType.MESH)

    def each(n, body):
        def step(i, carry):
            body(i)
            return carry

        lax.fori_loop(0, n, step, 0)

    def mixed(first, second, which):
        return tuple(a + (b - a) * which for a, b in zip(first, second))

    def pick(i, which):
        return mixed(EVEN[min(i, 14)], ODD[i], which)

    def slot(o, sign):
        a, y, x = o
        return ((zl + a) % 2) * 16 + ((yy + sign * y + 4) % 4) * 4 + (xx + sign * x + 4) % 4

    def plane(e, sign):
        return ((yy + sign * (e // 4) + 4) % 4) * 4 + (xx + sign * (e % 4) + 4) % 4

    def mate(o):
        zz = (z + o[0] * (1 - 2 * zl) + 8) % 8
        return (slot(o, 1), (zz // 2) * 2 + core)

    barrier = pltpu.get_barrier_semaphore()
    for i in range(15):
        signal(mate(pick(i, core)))

    @pl.when(core == 1)
    def _():
        signal(mate(ODD[15]))

    plane_even = [o for o in EVEN if o[0] == 0]
    plane_odd = [o for o in ODD if o[0] == 0]
    for i in range(7):
        signal(mate(mixed(plane_odd[i], plane_even[i], core)))

    @pl.when(core == 0)
    def _():
        signal(mate(plane_odd[7]))

    for d in range(1, 8):
        zz = (z + d) % 8
        signal(((zz % 2) * 16 + p % 16, (zz // 2) * 2 + zl))

    @pl.when(core != zl)
    def _():
        signal(sibling)

    signal(sibling)

    c_mom = pltpu.make_async_copy(mom.at[:, pl.ds(0, 128)], momv, in_sem.at[0])
    c_freq = pltpu.make_async_copy(freq, freqv, in_sem.at[1])
    c_tab = pltpu.make_async_copy(table.at[pl.ds(core * 16, 16)], tab, in_sem.at[2])
    c_own = pltpu.make_async_copy(prop, gs.at[p], in_sem.at[3])
    c_freq.start()

    def piece(i):
        rows = pl.ds(pl.multiple_of(i * 800, 800), 800)
        return pltpu.make_async_copy(vert.at[rows], vb.at[rows], v_sem.at[i])

    each(9, lambda i: piece(i).start())
    c_mom.start()
    c_own.start()
    c_tab.start()

    def widen(i):
        piece(i).wait()
        for t in range(5):
            rows = pl.ds(pl.multiple_of(i * 800 + t * 160, 160), 160)
            s32[rows, :] = vb[rows, :].astype(F32)

    each(9, widen)
    s32[pl.ds(7200, 64), :] = jnp.zeros((64, 128), F32)

    lane = lax.broadcasted_iota(I32, (8, 128), 1)
    c_freq.wait()

    def prepare(q):
        place = [(KQ * q) % 128 + freqv[w, 0] for w in range(2)]
        valid = [(lane + 256 - o) % 128 < 48 for o in place]
        for i in range(8):
            total = [None] * NB
            for w in range(2):
                blocks = {}
                for n2 in range(5):
                    off = 240 * i + 48 * n2
                    s, start = off // 128, off % 128
                    amount = (place[w] + (128 - start)) % 128
                    for n in range(5):
                        row = q * 900 + 180 * n + w + 2 * s
                        value = s32[pl.ds(row, 8, stride=30), :]
                        if start > 80:
                            after = s32[pl.ds(row + 2, 8, stride=30), :]
                            value = jnp.where(lane < start, after, value)
                        blocks[n, n2] = pltpu.roll(value, amount, 1)
                for f in range(NB):
                    term = None
                    for n, n2, sign in BLOCKS[f]:
                        if term is None:
                            term = blocks[n, n2]
                        elif sign > 0:
                            term = term + blocks[n, n2]
                        else:
                            term = term - blocks[n, n2]
                    term = jnp.where(valid[w], term, 0.0)
                    total[f] = term if total[f] is None else total[f] + term
            for f in range(NB):
                wown[q, pl.ds(48 * f + i, 6, stride=8), :] = total[f][0:6]

    each(NQ, prepare)
    c_own.wait()
    pl.semaphore_wait(barrier, 31 + core + zl - 2 * core * zl)

    def guard(i, which, body):
        if i < 15:
            body()
        else:
            pl.when(which == 1)(body)

    def ag(i):
        return remote(prop, gs.at[p], ag_s.at[i], ag_r.at[i], mate(pick(i, core)))

    def w_copy(q):
        return remote(wown.at[q], wrecv.at[q], w_s.at[q], w_r.at[q], sibling)

    def hand_on(i, which):
        block = slot(pick(i, which), -1)
        return remote(gs.at[block], gs.at[block], c_s.at[i], c_r.at[i], sibling)

    low = lax.broadcasted_iota(I32, (80, 128), 1) < 64

    def double(b):
        value = gs[b]
        turned = pltpu.roll(value, 64, 1)
        dup[2 * b] = jnp.where(low, value, turned)
        dup[2 * b + 1] = jnp.where(low, turned, value)

    for i in range(16):
        guard(i, core, lambda: ag(i).start())
    each(NQ, lambda q: w_copy(q).start())
    double(p)
    for i in reversed(range(16)):

        def pass_on():
            ag(i).wait_recv()
            hand_on(i, core).start()

        guard(i, core, pass_on)

    def settle(q):
        w_copy(q).wait_recv()

    each(NQ, settle)
    wide = lax.broadcasted_iota(I32, (48, 128), 1)

    def assemble(f):
        rows = pl.ds(pl.multiple_of(48 * f, 48), 48)
        tiles = [wown[q, rows, :] + wrecv[q, rows, :] for q in range(NQ)]
        for c in range(5):
            value = None
            for q in range(NQ):
                begin, end = KQ * q - 128 * c, KQ * (q + 1) - 128 * c
                if end <= 0 or begin >= 128:
                    continue
                value = tiles[q] if value is None else jnp.where(wide < begin, value, tiles[q])
            lhs[rows, 128 * c : 128 * c + 128] = value.astype(BF16)

    each(NB, assemble)
    for i in reversed(range(16)):
        guard(i, core, lambda: double(slot(pick(i, core), -1)))
    for i in reversed(range(16)):

        def receive():
            hand_on(i, other).wait_recv()
            double(slot(pick(i, other), -1))

        guard(i, other, receive)
    c_mom.wait()
    c_tab.wait()

    def build(step, ref):
        for half in range(2):
            x = 2 * (16 * core + plane(15 - 2 * step - half, 1))
            for q in range(NQ):
                shift = momv[q, 0]
                qx = shift // 64
                amount = (128 - shift % 64) % 128
                first = pltpu.roll(dup[(x + qx) % 64], amount, 1)
                second = pltpu.roll(dup[(x + 1 + qx) % 64], amount, 1)
                ref[KQ * q : KQ * q + 80, 128 * half : 128 * half + 128] = jnp.where(low, first, second)

    def s_copy(e):
        return remote(ssend.at[e], srecv.at[e], s_s.at[e], s_r.at[e], (zl * 16 + plane(e, 1), wa))

    def contract(step, ref):
        acc = jnp.dot(lhs[...], ref[...], preferred_element_type=F32)
        for half in range(2):
            e = 15 - 2 * step - half
            factors = tab[plane(e, 1)]
            flow = None
            for f in range(NB):
                term = factors[f : f + 1, :] * acc[48 * f : 48 * f + 48, 128 * half : 128 * half + 128]
                flow = term if flow is None else flow + term
            ssend[e] = flow

            @pl.when(e != 0)
            def _():
                s_copy(e).start()

    build(0, rhs0)

    def two(i):
        build(2 * i + 1, rhs1)
        contract(2 * i, rhs0)
        build((2 * i + 2) % 8, rhs0)
        contract(2 * i + 1, rhs1)

    each(4, two)

    red[...] = ssend[0]

    def gather_sum(i):
        e = 15 - i
        s_copy(e).wait_recv()
        red[...] += srecv[e]

    each(15, gather_sum)

    def f_copy(d):
        owner = 2 * ((wa // 2 + d // 2) % 4) + (core + d) % 2
        return remote(fsend.at[owner], frecv.at[z], f_s.at[d], f_r.at[z], (core * 16 + p % 16, owner))

    def f_arrival(d):
        k = (z + d) % 8
        return remote(fsend.at[0], frecv.at[k], f_s.at[0], f_r.at[k], ((k % 2) * 16 + p % 16, (k // 2) * 2 + zl))

    for j in range(8):
        fsend[j, 0:6, :] = red[6 * j : 6 * j + 6, :]
    for d in (4, 5, 2, 3, 6, 7, 1):
        f_copy(d).start()

    @pl.when(core != zl)
    def _():
        f_copy(0).start()
        f_arrival(0).wait_recv()

    @pl.when(core == zl)
    def _():
        frecv[z] = fsend[wa]

    for d in (1, 7, 2, 6, 3, 5, 4):
        f_arrival(d).wait_recv()
    total = frecv[0]
    for k in range(1, 8):
        total = total + frecv[k]
    out[...] = total[0:6]

    for i in range(16):

        def drain():
            ag(i).wait_send()
            hand_on(i, core).wait_send()

        guard(i, core, drain)
    each(NQ, lambda q: w_copy(q).wait_send())
    each(15, lambda i: s_copy(i + 1).wait_send())
    for d in range(1, 8):
        f_copy(d).wait_send()

    @pl.when(core != zl)
    def _():
        f_copy(0).wait_send()


def local(propagator, vertex, momentum_shift, frequency_shift):
    rows = vertex.transpose(0, 2, 1).reshape(3600, 128, 2).transpose(0, 2, 1).reshape(7200, 128)
    dma = pltpu.SemaphoreType.DMA
    vmem = pltpu.VMEM
    scratch = [
        vmem((7200, 128), BF16),
        vmem((7264, 128), F32),
        vmem((NQ, ROWS, 128), F32),
        vmem((NQ, ROWS, 128), F32),
        vmem((ROWS, NQ * KQ), BF16),
        vmem((32, 80, 128), BF16),
        vmem((64, 80, 128), BF16),
        vmem((NQ * KQ, 256), BF16),
        vmem((NQ * KQ, 256), BF16),
        vmem((16, 16, 128), F32),
        pltpu.SMEM((8, 128), I32),
        pltpu.SMEM((2, 48), I32),
        vmem((16, 48, 128), F32),
        vmem((16, 48, 128), F32),
        vmem((48, 128), F32),
        vmem((8, 8, 128), F32),
        vmem((8, 8, 128), F32),
        dma((4,)),
        dma((9,)),
    ]
    scratch += [dma((8,))] * 4 + [dma((16,))] * 6
    return pl.pallas_call(
        kernel,
        out_shape=jax.ShapeDtypeStruct((6, 128), F32),
        in_specs=[pl.BlockSpec(memory_space=pltpu.HBM)] * 5,
        out_specs=pl.BlockSpec(memory_space=pltpu.VMEM),
        scratch_shapes=scratch,
        compiler_params=pltpu.CompilerParams(
            collective_id=0, has_side_effects=True, vmem_limit_bytes=62 * 1024 * 1024
        ),
    )(propagator, rows, momentum_shift, frequency_shift, jnp.asarray(minus_functions()))


def solution(mesh):
    from jax.sharding import PartitionSpec as P

    in_specs = (P(None, "pb"), P("pb", "wa", None), P("pb", None), P("wa", None))
    out_specs = P("wa", "pb")
    return jax.shard_map(local, mesh=mesh, in_specs=in_specs, out_specs=out_specs, check_vma=False)
```

```python
import math

import jax
import jax.numpy as jnp
import numpy as np
from jax import lax
from jax.experimental import pallas as pl
from jax.experimental.pallas import tpu as pltpu

LAT = 64
F32 = jnp.float32
BF16 = jnp.bfloat16
I32 = jnp.int32
NQ = 8
NB = 13
ROWS = NB * 48
KQ = 80
DIST = (0, 1, 2, 1)
ORDER = (10, 9, 11, 6, 14, 8, 2, 5, 7, 13, 15, 1, 3, 4, 12, 0)

OFFSETS = sorted(
    ((a, y, x) for a in range(2) for y in range(4) for x in range(4) if a + y + x),
    key=lambda o: -(o[0] + DIST[o[1]] + DIST[o[2]]),
)
EVEN = [o for o in OFFSETS if sum(o) % 2 == 0]
ODD = [o for o in OFFSETS if sum(o) % 2 == 1]

BLOCKS = (
    ((0, 0, 1), (1, 1, 1), (2, 2, 1), (3, 3, 1), (4, 4, 1)),
    ((0, 1, 1), (1, 0, 1)),
    ((0, 2, 1), (2, 0, 1)),
    ((0, 3, 1), (3, 0, 1)),
    ((0, 4, 1), (4, 0, 1)),
    ((1, 1, 1), (3, 3, -1)),
    ((1, 3, 1), (3, 1, 1)),
    ((2, 2, 1), (4, 4, -1)),
    ((2, 4, 1), (4, 2, 1)),
    ((1, 2, 1), (2, 1, 1)),
    ((1, 4, 1), (4, 1, 1)),
    ((2, 3, 1), (3, 2, 1)),
    ((3, 4, 1), (4, 3, 1)),
)


def minus_functions():
    k = np.arange(LAT * LAT)
    a = (k // LAT) * (2.0 * math.pi / LAT)
    b = (k % LAT) * (2.0 * math.pi / LAT)
    root = math.sqrt(2.0)
    ca, cb, sa, sb = np.cos(a), np.cos(b), np.sin(a), np.sin(b)
    rows = [
        np.ones_like(a),
        root * ca,
        root * cb,
        root * sa,
        root * sb,
        np.cos(2 * a),
        np.sin(2 * a),
        np.cos(2 * b),
        np.sin(2 * b),
        2 * ca * cb,
        2 * ca * sb,
        2 * cb * sa,
        2 * sa * sb,
    ]
    table = np.zeros((16, LAT * LAT), np.float32)
    table[:NB] = -np.stack(rows)
    return np.ascontiguousarray(table.reshape(16, 32, 128).transpose(1, 0, 2))


def kernel(
    prop, vert, mom, freq, table, out,
    vb, s32, wown, wrecv, lhs, gs, dup, rhs0, rhs1, tab, momv, freqv,
    ssend, srecv, red, fsend, frecv,
    in_sem, v_sem, w_s, w_r, f_s, f_r, ag_s, ag_r, c_s, c_r, s_s, s_r,
):
    p = lax.axis_index("pb")
    wa = lax.axis_index("wa")
    zl = p // 16
    yy = (p // 4) % 4
    xx = p % 4
    core = wa % 2
    z = (wa // 2) * 2 + zl
    other = 1 - core
    sibling = (p, (wa // 2) * 2 + other)

    def remote(src, dst, send, recv, device):
        return pltpu.make_async_remote_copy(
            src_ref=src, dst_ref=dst, send_sem=send, recv_sem=recv,
            device_id=device, device_id_type=pl.DeviceIdType.MESH,
        )

    def signal(device):
        pl.semaphore_signal(barrier, inc=1, device_id=device, device_id_type=pl.DeviceIdType.MESH)

    def each(n, body):
        def step(i, carry):
            body(i)
            return carry

        lax.fori_loop(0, n, step, 0)

    def mixed(first, second, which):
        return tuple(a + (b - a) * which for a, b in zip(first, second))

    def pick(i, which):
        return mixed(EVEN[min(i, 14)], ODD[i], which)

    def slot(o, sign):
        a, y, x = o
        return ((zl + a) % 2) * 16 + ((yy + sign * y + 4) % 4) * 4 + (xx + sign * x + 4) % 4

    def plane(e, sign):
        return ((yy + sign * (e // 4) + 4) % 4) * 4 + (xx + sign * (e % 4) + 4) % 4

    def mate(o):
        zz = (z + o[0] * (1 - 2 * zl) + 8) % 8
        return (slot(o, 1), (zz // 2) * 2 + core)

    barrier = pltpu.get_barrier_semaphore()
    for i in range(15):
        signal(mate(pick(i, core)))

    @pl.when(core == 1)
    def _():
        signal(mate(ODD[15]))

    plane_even = [o for o in EVEN if o[0] == 0]
    plane_odd = [o for o in ODD if o[0] == 0]
    for i in range(7):
        signal(mate(mixed(plane_odd[i], plane_even[i], core)))

    @pl.when(core == 0)
    def _():
        signal(mate(plane_odd[7]))

    for d in range(1, 8):
        zz = (z + d) % 8
        signal(((zz % 2) * 16 + p % 16, (zz // 2) * 2 + zl))

    @pl.when(core != zl)
    def _():
        signal(sibling)

    signal(sibling)

    c_mom = pltpu.make_async_copy(mom.at[:, pl.ds(0, 128)], momv, in_sem.at[0])
    c_freq = pltpu.make_async_copy(freq, freqv, in_sem.at[1])
    c_tab = pltpu.make_async_copy(table.at[pl.ds(core * 16, 16)], tab, in_sem.at[2])
    c_own = pltpu.make_async_copy(prop, gs.at[p], in_sem.at[3])
    c_freq.start()

    def piece(i):
        rows = pl.ds(pl.multiple_of(i * 800, 800), 800)
        return pltpu.make_async_copy(vert.at[rows], vb.at[rows], v_sem.at[i])

    each(9, lambda i: piece(i).start())
    c_mom.start()
    c_own.start()
    c_tab.start()

    def widen(i):
        piece(i).wait()
        for t in range(5):
            rows = pl.ds(pl.multiple_of(i * 800 + t * 160, 160), 160)
            s32[rows, :] = vb[rows, :].astype(F32)

    each(9, widen)
    s32[pl.ds(7200, 64), :] = jnp.zeros((64, 128), F32)

    lane = lax.broadcasted_iota(I32, (8, 128), 1)
    c_freq.wait()

    def prepare(q):
        place = [(KQ * q) % 128 + freqv[w, 0] for w in range(2)]
        valid = [(lane + 256 - o) % 128 < 48 for o in place]
        for i in range(8):
            total = [None] * NB
            for w in range(2):
                blocks = {}
                for n2 in range(5):
                    off = 240 * i + 48 * n2
                    s, start = off // 128, off % 128
                    amount = (place[w] + (128 - start)) % 128
                    for n in range(5):
                        row = q * 900 + 180 * n + w + 2 * s
                        value = s32[pl.ds(row, 8, stride=30), :]
                        if start > 80:
                            after = s32[pl.ds(row + 2, 8, stride=30), :]
                            value = jnp.where(lane < start, after, value)
                        blocks[n, n2] = pltpu.roll(value, amount, 1)
                for f in range(NB):
                    term = None
                    for n, n2, sign in BLOCKS[f]:
                        if term is None:
                            term = blocks[n, n2]
                        elif sign > 0:
                            term = term + blocks[n, n2]
                        else:
                            term = term - blocks[n, n2]
                    term = jnp.where(valid[w], term, 0.0)
                    total[f] = term if total[f] is None else total[f] + term
            for f in range(NB):
                wown[q, pl.ds(48 * f + i, 6, stride=8), :] = total[f][0:6]

    c_own.wait()
    pl.semaphore_wait(barrier, 31 + core + zl - 2 * core * zl)

    def guard(i, which, body):
        if i < 15:
            body()
        else:
            pl.when(which == 1)(body)

    def ag(i):
        return remote(prop, gs.at[p], ag_s.at[i], ag_r.at[i], mate(pick(i, core)))

    def w_copy(q):
        return remote(wown.at[q], wrecv.at[q], w_s.at[q], w_r.at[q], sibling)

    def hand_on(i, which):
        block = slot(pick(i, which), -1)
        return remote(gs.at[block], gs.at[block], c_s.at[i], c_r.at[i], sibling)

    low = lax.broadcasted_iota(I32, (80, 128), 1) < 64

    def double(b):
        value = gs[b]
        turned = pltpu.roll(value, 64, 1)
        dup[2 * b] = jnp.where(low, value, turned)
        dup[2 * b + 1] = jnp.where(low, turned, value)

    for i in range(16):
        guard(i, core, lambda: ag(i).start())

    def prepare_and_send(q):
        prepare(q)
        w_copy(q).start()

    each(NQ, prepare_and_send)
    double(p)
    for i in reversed(range(16)):

        def pass_on():
            ag(i).wait_recv()
            hand_on(i, core).start()

        guard(i, core, pass_on)

    def settle(q):
        w_copy(q).wait_recv()

    each(NQ, settle)
    wide = lax.broadcasted_iota(I32, (48, 128), 1)

    def assemble(f):
        rows = pl.ds(pl.multiple_of(48 * f, 48), 48)
        tiles = [wown[q, rows, :] + wrecv[q, rows, :] for q in range(NQ)]
        for c in range(5):
            value = None
            for q in range(NQ):
                begin, end = KQ * q - 128 * c, KQ * (q + 1) - 128 * c
                if end <= 0 or begin >= 128:
                    continue
                value = tiles[q] if value is None else jnp.where(wide < begin, value, tiles[q])
            lhs[rows, 128 * c : 128 * c + 128] = value.astype(BF16)

    each(NB, assemble)
    for i in reversed(range(16)):
        guard(i, core, lambda: double(slot(pick(i, core), -1)))
    for i in reversed(range(16)):

        def receive():
            hand_on(i, other).wait_recv()
            double(slot(pick(i, other), -1))

        guard(i, other, receive)
    c_mom.wait()
    c_tab.wait()

    def build(step):
        ref = rhs[step % 2]
        for part in range(4):
            x = 2 * (16 * core + plane(ORDER[4 * step + part], 1))
            for q in range(NQ):
                shift = momv[q, 0]
                qx = shift // 64
                amount = (128 - shift % 64) % 128
                first = pltpu.roll(dup[(x + qx) % 64], amount, 1)
                second = pltpu.roll(dup[(x + 1 + qx) % 64], amount, 1)
                ref[KQ * q : KQ * q + 80, 128 * part : 128 * part + 128] = jnp.where(low, first, second)

    def s_copy(e):
        return remote(ssend.at[e], srecv.at[e], s_s.at[e], s_r.at[e], (zl * 16 + plane(e, 1), wa))

    def contract(step):
        acc = jnp.dot(lhs[...], rhs[step % 2][...], preferred_element_type=F32)
        for part in range(4):
            e = ORDER[4 * step + part]
            factors = tab[plane(e, 1)]
            flow = None
            for f in range(NB):
                term = factors[f : f + 1, :] * acc[48 * f : 48 * f + 48, 128 * part : 128 * part + 128]
                flow = term if flow is None else flow + term
            ssend[e] = flow
            if e:
                s_copy(e).start()

    rhs = (rhs0, rhs1)
    build(0)
    for step in range(4):
        if step < 3:
            build(step + 1)
        contract(step)

    red[...] = ssend[0]

    for e in ORDER[:15]:
        s_copy(e).wait_recv()
        red[...] += srecv[e]

    def f_copy(d):
        owner = 2 * ((wa // 2 + d // 2) % 4) + (core + d) % 2
        return remote(fsend.at[owner], frecv.at[z], f_s.at[d], f_r.at[z], (core * 16 + p % 16, owner))

    def f_arrival(d):
        k = (z + d) % 8
        return remote(fsend.at[0], frecv.at[k], f_s.at[0], f_r.at[k], ((k % 2) * 16 + p % 16, (k // 2) * 2 + zl))

    for j in range(8):
        fsend[j, 0:6, :] = red[6 * j : 6 * j + 6, :]
    for d in (4, 5, 2, 3, 6, 7, 1):
        f_copy(d).start()

    @pl.when(core != zl)
    def _():
        f_copy(0).start()
        f_arrival(0).wait_recv()

    @pl.when(core == zl)
    def _():
        frecv[z] = fsend[wa]

    for i in range(16):

        def drain():
            ag(i).wait_send()
            hand_on(i, core).wait_send()

        guard(i, core, drain)
    each(NQ, lambda q: w_copy(q).wait_send())
    each(15, lambda i: s_copy(i + 1).wait_send())

    for d in (1, 7, 2, 6, 3, 5, 4):
        f_arrival(d).wait_recv()
    total = frecv[0]
    for k in range(1, 8):
        total = total + frecv[k]
    for d in range(1, 8):
        f_copy(d).wait_send()

    @pl.when(core != zl)
    def _():
        f_copy(0).wait_send()
    out[...] = total[0:6]


def local(propagator, vertex, momentum_shift, frequency_shift):
    rows = vertex.transpose(0, 2, 1).reshape(3600, 128, 2).transpose(0, 2, 1).reshape(7200, 128)
    dma = pltpu.SemaphoreType.DMA
    vmem = pltpu.VMEM
    scratch = [
        vmem((7200, 128), BF16),
        vmem((7264, 128), F32),
        vmem((NQ, ROWS, 128), F32),
        vmem((NQ, ROWS, 128), F32),
        vmem((ROWS, NQ * KQ), BF16),
        vmem((32, 80, 128), BF16),
        vmem((64, 80, 128), BF16),
        vmem((NQ * KQ, 512), BF16),
        vmem((NQ * KQ, 512), BF16),
        vmem((16, 16, 128), F32),
        pltpu.SMEM((8, 128), I32),
        pltpu.SMEM((2, 48), I32),
        vmem((16, 48, 128), F32),
        vmem((16, 48, 128), F32),
        vmem((48, 128), F32),
        vmem((8, 8, 128), F32),
        vmem((8, 8, 128), F32),
        dma((4,)),
        dma((9,)),
    ]
    scratch += [dma((8,))] * 4 + [dma((16,))] * 6
    return pl.pallas_call(
        kernel,
        out_shape=jax.ShapeDtypeStruct((6, 128), F32),
        in_specs=[pl.BlockSpec(memory_space=pltpu.HBM)] * 5,
        out_specs=pl.BlockSpec(memory_space=pltpu.VMEM),
        scratch_shapes=scratch,
        compiler_params=pltpu.CompilerParams(
            collective_id=0, has_side_effects=True, vmem_limit_bytes=56549376
        ),
    )(propagator, rows, momentum_shift, frequency_shift, jnp.asarray(minus_functions()))


def solution(mesh):
    from jax.sharding import PartitionSpec as P

    in_specs = (P(None, "pb"), P("pb", "wa", None), P("pb", None), P("wa", None))
    out_specs = P("wa", "pb")
    return jax.shard_map(local, mesh=mesh, in_specs=in_specs, out_specs=out_specs, check_vma=False)
```

```python
import math

import jax
import jax.numpy as jnp
import numpy as np
from jax import lax
from jax.experimental import pallas as pl
from jax.experimental.pallas import tpu as pltpu

LAT = 64
F32 = jnp.float32
BF16 = jnp.bfloat16
I32 = jnp.int32
NQ = 8
NB = 13
ROWS = NB * 48
KQ = 80
DIST = (0, 1, 2, 1)
BITS = 14.0
ORDER = (10, 9, 11, 6, 14, 8, 2, 5, 7, 13, 15, 1, 3, 4, 12, 0)

OFFSETS = sorted(
    ((a, y, x) for a in range(2) for y in range(4) for x in range(4) if a + y + x),
    key=lambda o: -(o[0] + DIST[o[1]] + DIST[o[2]]),
)
EVEN = [o for o in OFFSETS if sum(o) % 2 == 0]
ODD = [o for o in OFFSETS if sum(o) % 2 == 1]

BLOCKS = (
    ((0, 0, 1), (1, 1, 1), (2, 2, 1), (3, 3, 1), (4, 4, 1)),
    ((0, 1, 1), (1, 0, 1)),
    ((0, 2, 1), (2, 0, 1)),
    ((0, 3, 1), (3, 0, 1)),
    ((0, 4, 1), (4, 0, 1)),
    ((1, 1, 1), (3, 3, -1)),
    ((1, 3, 1), (3, 1, 1)),
    ((2, 2, 1), (4, 4, -1)),
    ((2, 4, 1), (4, 2, 1)),
    ((1, 2, 1), (2, 1, 1)),
    ((1, 4, 1), (4, 1, 1)),
    ((2, 3, 1), (3, 2, 1)),
    ((3, 4, 1), (4, 3, 1)),
)


def minus_functions():
    k = np.arange(LAT * LAT)
    a = (k // LAT) * (2.0 * math.pi / LAT)
    b = (k % LAT) * (2.0 * math.pi / LAT)
    root = math.sqrt(2.0)
    ca, cb, sa, sb = np.cos(a), np.cos(b), np.sin(a), np.sin(b)
    rows = [
        np.ones_like(a),
        root * ca,
        root * cb,
        root * sa,
        root * sb,
        np.cos(2 * a),
        np.sin(2 * a),
        np.cos(2 * b),
        np.sin(2 * b),
        2 * ca * cb,
        2 * ca * sb,
        2 * cb * sa,
        2 * sa * sb,
    ]
    table = np.zeros((16, LAT * LAT), np.float32)
    table[:NB] = -np.stack(rows)
    return np.ascontiguousarray(table.reshape(16, 32, 128).transpose(1, 0, 2))


def kernel(
    prop, vert, mom, freq, table, out,
    vb, s32, wown, wrecv, lhs, gs, dup, rhs0, rhs1, tab, momv, freqv,
    ssend, srecv, red, fsend, frecv,
    in_sem, v_sem, w_s, w_r, f_s, f_r, ag_s, ag_r, c_s, c_r, s_s, s_r,
):
    p = lax.axis_index("pb")
    wa = lax.axis_index("wa")
    zl = p // 16
    yy = (p // 4) % 4
    xx = p % 4
    core = wa % 2
    z = (wa // 2) * 2 + zl
    other = 1 - core
    sibling = (p, (wa // 2) * 2 + other)

    def remote(src, dst, send, recv, device):
        return pltpu.make_async_remote_copy(
            src_ref=src, dst_ref=dst, send_sem=send, recv_sem=recv,
            device_id=device, device_id_type=pl.DeviceIdType.MESH,
        )

    def signal(device):
        pl.semaphore_signal(barrier, inc=1, device_id=device, device_id_type=pl.DeviceIdType.MESH)

    def each(n, body):
        def step(i, carry):
            body(i)
            return carry

        lax.fori_loop(0, n, step, 0)

    def mixed(first, second, which):
        return tuple(a + (b - a) * which for a, b in zip(first, second))

    def pick(i, which):
        return mixed(EVEN[min(i, 14)], ODD[i], which)

    def slot(o, sign):
        a, y, x = o
        return ((zl + a) % 2) * 16 + ((yy + sign * y + 4) % 4) * 4 + (xx + sign * x + 4) % 4

    def plane(e, sign):
        return ((yy + sign * (e // 4) + 4) % 4) * 4 + (xx + sign * (e % 4) + 4) % 4

    def mate(o):
        zz = (z + o[0] * (1 - 2 * zl) + 8) % 8
        return (slot(o, 1), (zz // 2) * 2 + core)

    barrier = pltpu.get_barrier_semaphore()
    for i in range(15):
        signal(mate(pick(i, core)))

    @pl.when(core == 1)
    def _():
        signal(mate(ODD[15]))

    plane_even = [o for o in EVEN if o[0] == 0]
    plane_odd = [o for o in ODD if o[0] == 0]
    for i in range(7):
        signal(mate(mixed(plane_odd[i], plane_even[i], core)))

    @pl.when(core == 0)
    def _():
        signal(mate(plane_odd[7]))

    for d in range(1, 8):
        zz = (z + d) % 8
        signal(((zz % 2) * 16 + p % 16, (zz // 2) * 2 + zl))

    @pl.when(core != zl)
    def _():
        signal(sibling)

    signal(sibling)

    c_mom = pltpu.make_async_copy(mom.at[:, pl.ds(0, 128)], momv, in_sem.at[0])
    c_freq = pltpu.make_async_copy(freq, freqv, in_sem.at[1])
    c_tab = pltpu.make_async_copy(table.at[pl.ds(core * 16, 16)], tab, in_sem.at[2])
    c_own = pltpu.make_async_copy(prop, gs.at[p], in_sem.at[3])
    c_freq.start()

    def piece(i):
        rows = pl.ds(pl.multiple_of(i * 800, 800), 800)
        return pltpu.make_async_copy(vert.at[rows], vb.at[rows], v_sem.at[i])

    each(9, lambda i: piece(i).start())
    c_mom.start()
    c_own.start()
    c_tab.start()

    def widen(i):
        piece(i).wait()
        for t in range(5):
            rows = pl.ds(pl.multiple_of(i * 800 + t * 160, 160), 160)
            s32[rows, :] = vb[rows, :].astype(F32)

    each(9, widen)
    s32[pl.ds(7200, 64), :] = jnp.zeros((64, 128), F32)

    lane = lax.broadcasted_iota(I32, (8, 128), 1)
    c_freq.wait()

    def prepare(q):
        place = [(KQ * q) % 128 + freqv[w, 0] for w in range(2)]
        valid = [(lane + 256 - o) % 128 < 48 for o in place]
        for i in range(8):
            total = [None] * NB
            for w in range(2):
                blocks = {}
                for n2 in range(5):
                    off = 240 * i + 48 * n2
                    s, start = off // 128, off % 128
                    amount = (place[w] + (128 - start)) % 128
                    for n in range(5):
                        row = q * 900 + 180 * n + w + 2 * s
                        value = s32[pl.ds(row, 8, stride=30), :]
                        if start > 80:
                            after = s32[pl.ds(row + 2, 8, stride=30), :]
                            value = jnp.where(lane < start, after, value)
                        blocks[n, n2] = pltpu.roll(value, amount, 1)
                for f in range(NB):
                    term = None
                    for n, n2, sign in BLOCKS[f]:
                        if term is None:
                            term = blocks[n, n2]
                        elif sign > 0:
                            term = term + blocks[n, n2]
                        else:
                            term = term - blocks[n, n2]
                    term = jnp.where(valid[w], term, 0.0)
                    total[f] = term if total[f] is None else total[f] + term
            for f in range(NB):
                wown[q, pl.ds(48 * f + i, 6, stride=8), :] = total[f][0:6]

    c_own.wait()
    pl.semaphore_wait(barrier, 31 + core + zl - 2 * core * zl)

    def guard(i, which, body):
        if i < 15:
            body()
        else:
            pl.when(which == 1)(body)

    def ag(i):
        return remote(prop, gs.at[p], ag_s.at[i], ag_r.at[i], mate(pick(i, core)))

    def w_copy(q):
        return remote(wown.at[q], wrecv.at[q], w_s.at[q], w_r.at[q], sibling)

    def hand_on(i, which):
        block = slot(pick(i, which), -1)
        return remote(gs.at[block], gs.at[block], c_s.at[i], c_r.at[i], sibling)

    low = lax.broadcasted_iota(I32, (80, 128), 1) < 64

    def double(b):
        value = gs[b]
        turned = pltpu.roll(value, 64, 1)
        dup[2 * b] = jnp.where(low, value, turned)
        dup[2 * b + 1] = jnp.where(low, turned, value)

    for i in range(16):
        guard(i, core, lambda: ag(i).start())

    def prepare_and_send(q):
        prepare(q)
        w_copy(q).start()

    each(NQ, prepare_and_send)
    double(p)
    for i in reversed(range(16)):

        def pass_on():
            ag(i).wait_recv()
            hand_on(i, core).start()

        guard(i, core, pass_on)

    def settle(q):
        w_copy(q).wait_recv()

    each(NQ, settle)
    wide = lax.broadcasted_iota(I32, (48, 128), 1)

    def assemble(f):
        rows = pl.ds(pl.multiple_of(48 * f, 48), 48)
        tiles = [wown[q, rows, :] + wrecv[q, rows, :] for q in range(NQ)]
        for c in range(5):
            value = None
            for q in range(NQ):
                begin, end = KQ * q - 128 * c, KQ * (q + 1) - 128 * c
                if end <= 0 or begin >= 128:
                    continue
                value = tiles[q] if value is None else jnp.where(wide < begin, value, tiles[q])
            lhs[rows, 128 * c : 128 * c + 128] = value.astype(BF16)

    each(NB, assemble)
    for i in reversed(range(16)):
        guard(i, core, lambda: double(slot(pick(i, core), -1)))
    for i in reversed(range(16)):

        def receive():
            hand_on(i, other).wait_recv()
            double(slot(pick(i, other), -1))

        guard(i, other, receive)
    c_mom.wait()
    c_tab.wait()

    def build(step):
        ref = rhs[step % 2]
        for part in range(4):
            x = 2 * (16 * core + plane(ORDER[4 * step + part], 1))
            for q in range(NQ):
                shift = momv[q, 0]
                qx = shift // 64
                amount = (128 - shift % 64) % 128
                first = pltpu.roll(dup[(x + qx) % 64], amount, 1)
                second = pltpu.roll(dup[(x + 1 + qx) % 64], amount, 1)
                ref[KQ * q : KQ * q + 80, 128 * part : 128 * part + 128] = jnp.where(low, first, second)

    def encode(flow, ref):
        top = jnp.abs(flow[0:8])
        for t in range(1, 6):
            top = jnp.maximum(top, jnp.abs(flow[8 * t : 8 * t + 8]))
        power = jnp.floor(jnp.log2(jnp.maximum(top, 2.0**-100))) + 1.0
        unit = jnp.exp2(BITS - power)
        parts = [jnp.round(flow[8 * t : 8 * t + 8] * unit) for t in range(6)]
        ref[...] = jnp.concatenate(parts + [power, power], axis=0).astype(I32).astype(jnp.int16)

    def decode(ref):
        values = ref[...].astype(I32).astype(F32)
        unit = jnp.exp2(values[48:56] - BITS)
        for t in range(6):
            red[8 * t : 8 * t + 8, :] += values[8 * t : 8 * t + 8] * unit

    def s_copy(e):
        return remote(ssend.at[e], srecv.at[e], s_s.at[e], s_r.at[e], (zl * 16 + plane(e, 1), wa))

    def contract(step):
        acc = jnp.dot(lhs[...], rhs[step % 2][...], preferred_element_type=F32)
        for part in range(4):
            e = ORDER[4 * step + part]
            factors = tab[plane(e, 1)]
            flow = None
            for f in range(NB):
                term = factors[f : f + 1, :] * acc[48 * f : 48 * f + 48, 128 * part : 128 * part + 128]
                flow = term if flow is None else flow + term
            if e:
                encode(flow, ssend.at[e])
                s_copy(e).start()
            else:
                red[...] = flow

    rhs = (rhs0, rhs1)
    build(0)
    for step in range(4):
        if step < 3:
            build(step + 1)
        contract(step)

    for e in ORDER[:15]:
        s_copy(e).wait_recv()
        decode(srecv.at[e])

    def f_copy(d):
        owner = 2 * ((wa // 2 + d // 2) % 4) + (core + d) % 2
        return remote(fsend.at[owner], frecv.at[z], f_s.at[d], f_r.at[z], (core * 16 + p % 16, owner))

    def f_arrival(d):
        k = (z + d) % 8
        return remote(fsend.at[0], frecv.at[k], f_s.at[0], f_r.at[k], ((k % 2) * 16 + p % 16, (k // 2) * 2 + zl))

    for j in range(8):
        fsend[j, 0:6, :] = red[6 * j : 6 * j + 6, :]
    for d in (4, 5, 2, 3, 6, 7, 1):
        f_copy(d).start()

    @pl.when(core != zl)
    def _():
        f_copy(0).start()
        f_arrival(0).wait_recv()

    @pl.when(core == zl)
    def _():
        frecv[z] = fsend[wa]

    for i in range(16):

        def drain():
            ag(i).wait_send()
            hand_on(i, core).wait_send()

        guard(i, core, drain)
    each(NQ, lambda q: w_copy(q).wait_send())
    each(15, lambda i: s_copy(i + 1).wait_send())

    for d in (1, 7, 2, 6, 3, 5, 4):
        f_arrival(d).wait_recv()
    total = frecv[0]
    for k in range(1, 8):
        total = total + frecv[k]
    for d in range(1, 8):
        f_copy(d).wait_send()

    @pl.when(core != zl)
    def _():
        f_copy(0).wait_send()
    out[...] = total[0:6]


def local(propagator, vertex, momentum_shift, frequency_shift):
    rows = vertex.transpose(0, 2, 1).reshape(3600, 128, 2).transpose(0, 2, 1).reshape(7200, 128)
    dma = pltpu.SemaphoreType.DMA
    vmem = pltpu.VMEM
    scratch = [
        vmem((7200, 128), BF16),
        vmem((7264, 128), F32),
        vmem((NQ, ROWS, 128), F32),
        vmem((NQ, ROWS, 128), F32),
        vmem((ROWS, NQ * KQ), BF16),
        vmem((32, 80, 128), BF16),
        vmem((64, 80, 128), BF16),
        vmem((NQ * KQ, 512), BF16),
        vmem((NQ * KQ, 512), BF16),
        vmem((16, 16, 128), F32),
        pltpu.SMEM((8, 128), I32),
        pltpu.SMEM((2, 48), I32),
        vmem((16, 64, 128), jnp.int16),
        vmem((16, 64, 128), jnp.int16),
        vmem((48, 128), F32),
        vmem((8, 8, 128), F32),
        vmem((8, 8, 128), F32),
        dma((4,)),
        dma((9,)),
    ]
    scratch += [dma((8,))] * 4 + [dma((16,))] * 6
    return pl.pallas_call(
        kernel,
        out_shape=jax.ShapeDtypeStruct((6, 128), F32),
        in_specs=[pl.BlockSpec(memory_space=pltpu.HBM)] * 5,
        out_specs=pl.BlockSpec(memory_space=pltpu.VMEM),
        scratch_shapes=scratch,
        compiler_params=pltpu.CompilerParams(
            collective_id=0, has_side_effects=True, vmem_limit_bytes=56549376
        ),
    )(propagator, rows, momentum_shift, frequency_shift, jnp.asarray(minus_functions()))


def solution(mesh):
    from jax.sharding import PartitionSpec as P

    in_specs = (P(None, "pb"), P("pb", "wa", None), P("pb", None), P("wa", None))
    out_specs = P("wa", "pb")
    return jax.shard_map(local, mesh=mesh, in_specs=in_specs, out_specs=out_specs, check_vma=False)
```

```python
import math

import jax
import jax.numpy as jnp
import numpy as np
from jax import lax
from jax.experimental import pallas as pl
from jax.experimental.pallas import tpu as pltpu

LAT = 64
F32 = jnp.float32
BF16 = jnp.bfloat16
I32 = jnp.int32
NQ = 8
NB = 13
ROWS = NB * 48
KQ = 80
BITS = 14.0
ORDER = (10, 9, 11, 14, 6, 8, 2, 13, 7, 5, 15, 4, 12, 1, 3, 0)

BLOCKS = (
    ((0, 0, 1), (1, 1, 1), (2, 2, 1), (3, 3, 1), (4, 4, 1)),
    ((0, 1, 1), (1, 0, 1)),
    ((0, 2, 1), (2, 0, 1)),
    ((0, 3, 1), (3, 0, 1)),
    ((0, 4, 1), (4, 0, 1)),
    ((1, 1, 1), (3, 3, -1)),
    ((1, 3, 1), (3, 1, 1)),
    ((2, 2, 1), (4, 4, -1)),
    ((2, 4, 1), (4, 2, 1)),
    ((1, 2, 1), (2, 1, 1)),
    ((1, 4, 1), (4, 1, 1)),
    ((2, 3, 1), (3, 2, 1)),
    ((3, 4, 1), (4, 3, 1)),
)


def minus_functions():
    k = np.arange(LAT * LAT)
    a = (k // LAT) * (2.0 * math.pi / LAT)
    b = (k % LAT) * (2.0 * math.pi / LAT)
    root = math.sqrt(2.0)
    ca, cb, sa, sb = np.cos(a), np.cos(b), np.sin(a), np.sin(b)
    rows = [
        np.ones_like(a),
        root * ca,
        root * cb,
        root * sa,
        root * sb,
        np.cos(2 * a),
        np.sin(2 * a),
        np.cos(2 * b),
        np.sin(2 * b),
        2 * ca * cb,
        2 * ca * sb,
        2 * cb * sa,
        2 * sa * sb,
    ]
    table = np.zeros((16, LAT * LAT), np.float32)
    table[:NB] = -np.stack(rows)
    return np.ascontiguousarray(table.reshape(16, 32, 128).transpose(1, 0, 2))


def kernel(
    prop, vert, mom, freq, table, out,
    vb, s32, wown, wrecv, lhs, gs, dup, rhs0, rhs1, tab, momv, freqv,
    ssend, srecv, red, fsend, frecv,
    in_sem, v_sem, w_s, w_r, f_s, f_r, ag_s, ag_r, c_s, c_r, s_s, s_r,
):
    p = lax.axis_index("pb")
    wa = lax.axis_index("wa")
    zl = p // 16
    yy = (p // 4) % 4
    xx = p % 4
    core = wa % 2
    z = (wa // 2) * 2 + zl
    other = 1 - core
    sibling = (p, (wa // 2) * 2 + other)

    def remote(src, dst, send, recv, device):
        return pltpu.make_async_remote_copy(
            src_ref=src, dst_ref=dst, send_sem=send, recv_sem=recv,
            device_id=device, device_id_type=pl.DeviceIdType.MESH,
        )

    def signal(device):
        pl.semaphore_signal(barrier, inc=1, device_id=device, device_id_type=pl.DeviceIdType.MESH)

    def each(n, body):
        def step(i, carry):
            body(i)
            return carry

        lax.fori_loop(0, n, step, 0)

    def pick(i, which):
        y = (i // 4 + 2) % 4
        x = (i % 4 + 2) % 4
        return ((which + y + x) % 2, y, x)

    def slot(o, sign):
        a, y, x = o
        return ((zl + a) % 2) * 16 + ((yy + sign * y + 4) % 4) * 4 + (xx + sign * x + 4) % 4

    def plane(e, sign):
        return ((yy + sign * (e // 4) + 4) % 4) * 4 + (xx + sign * (e % 4) + 4) % 4

    def mate(o):
        zz = (z + o[0] * (1 - 2 * zl) + 8) % 8
        return (slot(o, 1), (zz // 2) * 2 + core)

    barrier = pltpu.get_barrier_semaphore()
    def guard(i, which, body):
        pl.when((i != 10) | (which == 1))(body)

    each(16, lambda i: guard(i, core, lambda: signal(mate(pick(i, core)))))

    def greet_along(d):
        zz = (z + 1 + d) % 8
        signal(((zz % 2) * 16 + p % 16, (zz // 2) * 2 + zl))

    def greet_plane(i):
        y = (i // 2 + 2) % 4
        x = 2 * (i % 2) + (y + core + 1) % 2

        @pl.when(4 * y + x != 0)
        def _():
            signal(mate((0, y, x)))

    each(7, greet_along)
    each(8, greet_plane)

    @pl.when(core != zl)
    def _():
        signal(sibling)

    signal(sibling)

    c_mom = pltpu.make_async_copy(mom.at[:, pl.ds(0, 128)], momv, in_sem.at[0])
    c_freq = pltpu.make_async_copy(freq, freqv, in_sem.at[1])
    c_tab = pltpu.make_async_copy(table.at[pl.ds(core * 16, 16)], tab, in_sem.at[2])
    c_own = pltpu.make_async_copy(prop, gs.at[p], in_sem.at[3])
    c_freq.start()

    def piece(i):
        rows = pl.ds(pl.multiple_of(i * 800, 800), 800)
        return pltpu.make_async_copy(vert.at[rows], vb.at[rows], v_sem.at[i])

    each(9, lambda i: piece(i).start())
    c_mom.start()
    c_own.start()
    c_tab.start()

    def widen(i):
        piece(i).wait()
        for t in range(5):
            rows = pl.ds(pl.multiple_of(i * 800 + t * 160, 160), 160)
            s32[rows, :] = vb[rows, :].astype(F32)

    each(9, widen)
    s32[pl.ds(7200, 64), :] = jnp.zeros((64, 128), F32)

    lane = lax.broadcasted_iota(I32, (8, 128), 1)
    c_freq.wait()

    def prepare(q):
        place = [(KQ * q) % 128 + freqv[w, 0] for w in range(2)]
        valid = [(lane + 256 - o) % 128 < 48 for o in place]
        for i in range(8):
            total = [None] * NB
            for w in range(2):
                blocks = {}
                for n2 in range(5):
                    off = 240 * i + 48 * n2
                    s, start = off // 128, off % 128
                    amount = (place[w] + (128 - start)) % 128
                    for n in range(5):
                        row = q * 900 + 180 * n + w + 2 * s
                        value = s32[pl.ds(row, 8, stride=30), :]
                        if start > 80:
                            after = s32[pl.ds(row + 2, 8, stride=30), :]
                            value = jnp.where(lane < start, after, value)
                        blocks[n, n2] = pltpu.roll(value, amount, 1)
                for f in range(NB):
                    term = None
                    for n, n2, sign in BLOCKS[f]:
                        if term is None:
                            term = blocks[n, n2]
                        elif sign > 0:
                            term = term + blocks[n, n2]
                        else:
                            term = term - blocks[n, n2]
                    term = jnp.where(valid[w], term, 0.0)
                    total[f] = term if total[f] is None else total[f] + term
            for f in range(NB):
                wown[q, pl.ds(48 * f + i, 6, stride=8), :] = total[f][0:6]

    c_own.wait()
    pl.semaphore_wait(barrier, 31 + core + zl - 2 * core * zl)

    def ag(i):
        return remote(gs.at[p], gs.at[p], ag_s.at[i], ag_r.at[i], mate(pick(i, core)))

    def w_copy(q):
        return remote(wown.at[q], wrecv.at[q], w_s.at[q], w_r.at[q], sibling)

    def hand_on(i, which):
        block = slot(pick(i, which), -1)
        return remote(gs.at[block], gs.at[block], c_s.at[i], c_r.at[i], sibling)

    low = lax.broadcasted_iota(I32, (80, 128), 1) < 64

    def double(b):
        value = gs[b]
        turned = pltpu.roll(value, 64, 1)
        dup[2 * b] = jnp.where(low, value, turned)
        dup[2 * b + 1] = jnp.where(low, turned, value)

    each(16, lambda i: guard(i, core, lambda: ag(i).start()))

    def prepare_and_send(q):
        prepare(q)
        w_copy(q).start()

    each(NQ, prepare_and_send)
    double(p)
    def pass_on(n):
        i = 15 - n

        def body():
            ag(i).wait_recv()
            hand_on(i, core).start()

        guard(i, core, body)

    each(16, pass_on)

    def settle(q):
        w_copy(q).wait_recv()

    each(NQ, settle)
    wide = lax.broadcasted_iota(I32, (48, 128), 1)

    def assemble(f):
        rows = pl.ds(pl.multiple_of(48 * f, 48), 48)
        tiles = [wown[q, rows, :] + wrecv[q, rows, :] for q in range(NQ)]
        for c in range(5):
            value = None
            for q in range(NQ):
                begin, end = KQ * q - 128 * c, KQ * (q + 1) - 128 * c
                if end <= 0 or begin >= 128:
                    continue
                value = tiles[q] if value is None else jnp.where(wide < begin, value, tiles[q])
            lhs[rows, 128 * c : 128 * c + 128] = value.astype(BF16)

    each(NB, assemble)
    def double_own(n):
        for u in range(4):
            double(slot(pick(4 * n + u, core), -1))

    each(4, double_own)

    def receive(n):
        for u in range(4):
            i = 15 - 4 * n - u
            guard(i, other, hand_on(i, other).wait_recv)
        for u in range(4):
            double(slot(pick(15 - 4 * n - u, other), -1))

    each(4, receive)
    c_mom.wait()
    c_tab.wait()

    def build(step):
        ref = rhs[step % 2]
        for part in range(4):
            x = 2 * (16 * core + plane(ORDER[4 * step + part], 1))
            for q in range(NQ):
                shift = momv[q, 0]
                qx = shift // 64
                amount = (128 - shift % 64) % 128
                first = pltpu.roll(dup[(x + qx) % 64], amount, 1)
                second = pltpu.roll(dup[(x + 1 + qx) % 64], amount, 1)
                ref[KQ * q : KQ * q + 80, 128 * part : 128 * part + 128] = jnp.where(low, first, second)

    def encode(flow, ref):
        top = jnp.abs(flow[0:8])
        for t in range(1, 6):
            top = jnp.maximum(top, jnp.abs(flow[8 * t : 8 * t + 8]))
        power = jnp.floor(jnp.log2(jnp.maximum(top, 2.0**-100))) + 1.0
        unit = jnp.exp2(BITS - power)
        parts = [jnp.round(flow[8 * t : 8 * t + 8] * unit) for t in range(6)]
        ref[...] = jnp.concatenate(parts + [power, power], axis=0).astype(I32).astype(jnp.int16)

    def decode(ref):
        values = ref[...].astype(I32).astype(F32)
        unit = jnp.exp2(values[48:56] - BITS)
        return jnp.concatenate([values[8 * t : 8 * t + 8] * unit for t in range(6)], axis=0)

    def s_copy(e):
        return remote(ssend.at[e], srecv.at[e], s_s.at[e], s_r.at[e], (zl * 16 + plane(e, 1), wa))

    def contract(step):
        acc = jnp.dot(lhs[...], rhs[step % 2][...], preferred_element_type=F32)
        for part in range(4):
            e = ORDER[4 * step + part]
            factors = tab[plane(e, 1)]
            flow = None
            for f in range(NB):
                term = factors[f : f + 1, :] * acc[48 * f : 48 * f + 48, 128 * part : 128 * part + 128]
                flow = term if flow is None else flow + term
            if e:
                encode(flow, ssend.at[e])
            else:
                red[...] = flow
        for part in range(4):
            if ORDER[4 * step + part]:
                s_copy(ORDER[4 * step + part]).start()

    rhs = (rhs0, rhs1)
    build(0)
    for step in range(4):
        if step < 3:
            build(step + 1)
        contract(step)

    for group in (ORDER[0:11], ORDER[11:15]):
        for e in group:
            s_copy(e).wait_recv()
        flow = red[...]
        for e in group:
            flow = flow + decode(srecv.at[e])
        red[...] = flow

    def f_copy(d):
        owner = 2 * ((wa // 2 + d // 2) % 4) + (core + d) % 2
        return remote(fsend.at[owner], frecv.at[z], f_s.at[d], f_r.at[z], (core * 16 + p % 16, owner))

    def f_arrival(d):
        k = (z + d) % 8
        return remote(fsend.at[0], frecv.at[k], f_s.at[0], f_r.at[k], ((k % 2) * 16 + p % 16, (k // 2) * 2 + zl))

    for j in range(8):
        fsend[j, 0:6, :] = red[6 * j : 6 * j + 6, :]
    for d in (4, 5, 2, 3, 6, 7, 1):
        f_copy(d).start()

    @pl.when(core != zl)
    def _():
        f_copy(0).start()
        f_arrival(0).wait_recv()

    @pl.when(core == zl)
    def _():
        frecv[z] = fsend[wa]

    def drain(i):
        def body():
            ag(i).wait_send()
            hand_on(i, core).wait_send()

        guard(i, core, body)

    each(16, drain)
    each(NQ, lambda q: w_copy(q).wait_send())
    each(15, lambda i: s_copy(i + 1).wait_send())

    for d in range(1, 8):
        f_copy(d).wait_send()

    @pl.when(core != zl)
    def _():
        f_copy(0).wait_send()

    for d in (1, 7, 2, 6, 3, 5, 4):
        f_arrival(d).wait_recv()
    total = frecv[0]
    for k in range(1, 8):
        total = total + frecv[k]
    out[...] = total[0:6]


def local(propagator, vertex, momentum_shift, frequency_shift):
    rows = vertex.transpose(0, 2, 1).reshape(3600, 128, 2).transpose(0, 2, 1).reshape(7200, 128)
    dma = pltpu.SemaphoreType.DMA
    vmem = pltpu.VMEM
    scratch = [
        vmem((7200, 128), BF16),
        vmem((7264, 128), F32),
        vmem((NQ, ROWS, 128), F32),
        vmem((NQ, ROWS, 128), F32),
        vmem((ROWS, NQ * KQ), BF16),
        vmem((32, 80, 128), BF16),
        vmem((64, 80, 128), BF16),
        vmem((NQ * KQ, 512), BF16),
        vmem((NQ * KQ, 512), BF16),
        vmem((16, 16, 128), F32),
        pltpu.SMEM((8, 128), I32),
        pltpu.SMEM((2, 48), I32),
        vmem((16, 64, 128), jnp.int16),
        vmem((16, 64, 128), jnp.int16),
        vmem((48, 128), F32),
        vmem((8, 8, 128), F32),
        vmem((8, 8, 128), F32),
        dma((4,)),
        dma((9,)),
    ]
    scratch += [dma((8,))] * 4 + [dma((16,))] * 6
    return pl.pallas_call(
        kernel,
        out_shape=jax.ShapeDtypeStruct((6, 128), F32),
        in_specs=[pl.BlockSpec(memory_space=pltpu.HBM)] * 5,
        out_specs=pl.BlockSpec(memory_space=pltpu.VMEM),
        scratch_shapes=scratch,
        compiler_params=pltpu.CompilerParams(
            collective_id=0, has_side_effects=True, vmem_limit_bytes=56549376
        ),
    )(propagator, rows, momentum_shift, frequency_shift, jnp.asarray(minus_functions()))


def solution(mesh):
    from jax.sharding import PartitionSpec as P

    in_specs = (P(None, "pb"), P("pb", "wa", None), P("pb", None), P("wa", None))
    out_specs = P("wa", "pb")
    return jax.shard_map(local, mesh=mesh, in_specs=in_specs, out_specs=out_specs, check_vma=False)
```

```python
import math

import jax
import jax.numpy as jnp
import numpy as np
from jax import lax
from jax.experimental import pallas as pl
from jax.experimental.pallas import tpu as pltpu

LAT = 64
F32 = jnp.float32
BF16 = jnp.bfloat16
I32 = jnp.int32
NQ = 8
NB = 13
ROWS = NB * 48
KQ = 80
BITS = 14.0
ORDER = (10, 9, 11, 14, 6, 8, 2, 13, 7, 5, 15, 4, 12, 1, 3, 0)

BLOCKS = (
    ((0, 0, 1), (1, 1, 1), (2, 2, 1), (3, 3, 1), (4, 4, 1)),
    ((0, 1, 1), (1, 0, 1)),
    ((0, 2, 1), (2, 0, 1)),
    ((0, 3, 1), (3, 0, 1)),
    ((0, 4, 1), (4, 0, 1)),
    ((1, 1, 1), (3, 3, -1)),
    ((1, 3, 1), (3, 1, 1)),
    ((2, 2, 1), (4, 4, -1)),
    ((2, 4, 1), (4, 2, 1)),
    ((1, 2, 1), (2, 1, 1)),
    ((1, 4, 1), (4, 1, 1)),
    ((2, 3, 1), (3, 2, 1)),
    ((3, 4, 1), (4, 3, 1)),
)


def minus_functions():
    k = np.arange(LAT * LAT)
    a = (k // LAT) * (2.0 * math.pi / LAT)
    b = (k % LAT) * (2.0 * math.pi / LAT)
    root = math.sqrt(2.0)
    ca, cb, sa, sb = np.cos(a), np.cos(b), np.sin(a), np.sin(b)
    rows = [
        np.ones_like(a),
        root * ca,
        root * cb,
        root * sa,
        root * sb,
        np.cos(2 * a),
        np.sin(2 * a),
        np.cos(2 * b),
        np.sin(2 * b),
        2 * ca * cb,
        2 * ca * sb,
        2 * cb * sa,
        2 * sa * sb,
    ]
    table = np.zeros((16, LAT * LAT), np.float32)
    table[:NB] = -np.stack(rows)
    return np.ascontiguousarray(table.reshape(16, 32, 128).transpose(1, 0, 2))


def kernel(
    prop, vert, mom, freq, table, out,
    vb, s32, wown, wrecv, lhs, gs, dup, rhs0, rhs1, tab, momv, freqv,
    ssend, srecv, red, fsend, frecv,
    in_sem, v_sem, w_s, w_r, f_s, f_r, ag_s, ag_r, c_s, c_r, s_s, s_r,
):
    p = lax.axis_index("pb")
    wa = lax.axis_index("wa")
    zl = p // 16
    yy = (p // 4) % 4
    xx = p % 4
    core = wa % 2
    z = (wa // 2) * 2 + zl
    other = 1 - core
    sibling = (p, (wa // 2) * 2 + other)

    def remote(src, dst, send, recv, device):
        return pltpu.make_async_remote_copy(
            src_ref=src, dst_ref=dst, send_sem=send, recv_sem=recv,
            device_id=device, device_id_type=pl.DeviceIdType.MESH,
        )

    def signal(device):
        pl.semaphore_signal(barrier, inc=1, device_id=device, device_id_type=pl.DeviceIdType.MESH)

    def each(n, body):
        def step(i, carry):
            body(i)
            return carry

        lax.fori_loop(0, n, step, 0)

    def pick(i, which):
        y = (i // 4 + 2) % 4
        x = (i % 4 + 2) % 4
        return ((which + y + x) % 2, y, x)

    def slot(o, sign):
        a, y, x = o
        return ((zl + a) % 2) * 16 + ((yy + sign * y + 4) % 4) * 4 + (xx + sign * x + 4) % 4

    def plane(e, sign):
        return ((yy + sign * (e // 4) + 4) % 4) * 4 + (xx + sign * (e % 4) + 4) % 4

    def mate(o):
        zz = (z + o[0] * (1 - 2 * zl) + 8) % 8
        return (slot(o, 1), (zz // 2) * 2 + core)

    barrier = pltpu.get_barrier_semaphore()
    def guard(i, which, body):
        pl.when((i != 10) | (which == 1))(body)

    each(16, lambda i: guard(i, core, lambda: signal(mate(pick(i, core)))))

    def greet_along(d):
        zz = (z + 1 + d) % 8
        signal(((zz % 2) * 16 + p % 16, (zz // 2) * 2 + zl))

    def greet_plane(i):
        y = (i // 2 + 2) % 4
        x = 2 * (i % 2) + (y + core + 1) % 2

        @pl.when(4 * y + x != 0)
        def _():
            signal(mate((0, y, x)))

    each(7, greet_along)
    each(8, greet_plane)

    @pl.when(core != zl)
    def _():
        signal(sibling)

    signal(sibling)

    c_mom = pltpu.make_async_copy(mom.at[:, pl.ds(0, 128)], momv, in_sem.at[0])
    c_freq = pltpu.make_async_copy(freq, freqv, in_sem.at[1])
    c_tab = pltpu.make_async_copy(table.at[pl.ds(core * 16, 16)], tab, in_sem.at[2])
    c_own = pltpu.make_async_copy(prop, gs.at[p], in_sem.at[3])
    c_freq.start()

    def piece(i):
        rows = pl.ds(pl.multiple_of(i * 800, 800), 800)
        return pltpu.make_async_copy(vert.at[rows], vb.at[rows], v_sem.at[i])

    each(9, lambda i: piece(i).start())
    c_mom.start()
    c_own.start()
    c_tab.start()

    def widen(i):
        piece(i).wait()
        for t in range(5):
            rows = pl.ds(pl.multiple_of(i * 800 + t * 160, 160), 160)
            s32[rows, :] = vb[rows, :].astype(F32)

    each(9, widen)
    s32[pl.ds(7200, 64), :] = jnp.zeros((64, 128), F32)

    lane = lax.broadcasted_iota(I32, (8, 128), 1)
    c_freq.wait()

    def prepare(q):
        place = [(KQ * q) % 128 + freqv[w, 0] for w in range(2)]
        valid = [(lane + 256 - o) % 128 < 48 for o in place]
        for i in range(8):
            total = [None] * NB
            for w in range(2):
                blocks = {}
                for n2 in range(5):
                    off = 240 * i + 48 * n2
                    s, start = off // 128, off % 128
                    amount = (place[w] + (128 - start)) % 128
                    for n in range(5):
                        row = q * 900 + 180 * n + w + 2 * s
                        value = s32[pl.ds(row, 8, stride=30), :]
                        if start > 80:
                            after = s32[pl.ds(row + 2, 8, stride=30), :]
                            value = jnp.where(lane < start, after, value)
                        blocks[n, n2] = pltpu.roll(value, amount, 1)
                for f in range(NB):
                    term = None
                    for n, n2, sign in BLOCKS[f]:
                        if term is None:
                            term = blocks[n, n2]
                        elif sign > 0:
                            term = term + blocks[n, n2]
                        else:
                            term = term - blocks[n, n2]
                    term = jnp.where(valid[w], term, 0.0)
                    total[f] = term if total[f] is None else total[f] + term
            for f in range(NB):
                wown[q, pl.ds(48 * f + i, 6, stride=8), :] = total[f][0:6]

    c_own.wait()
    pl.semaphore_wait(barrier, 31 + core + zl - 2 * core * zl)

    def ag(i):
        return remote(gs.at[p], gs.at[p], ag_s.at[i], ag_r.at[i], mate(pick(i, core)))

    def w_copy(q):
        return remote(wown.at[q, pl.ds(0, ROWS)], wrecv.at[q], w_s.at[q], w_r.at[q], sibling)

    def hand_on(i, which):
        block = slot(pick(i, which), -1)
        return remote(gs.at[block], gs.at[block], c_s.at[i], c_r.at[i], sibling)

    low = lax.broadcasted_iota(I32, (80, 128), 1) < 64

    def double(b):
        value = gs[b]
        turned = pltpu.roll(value, 64, 1)
        dup[2 * b] = jnp.where(low, value, turned)
        dup[2 * b + 1] = jnp.where(low, turned, value)

    each(16, lambda i: guard(i, core, lambda: ag(i).start()))

    def prepare_and_send(q):
        prepare(q)
        w_copy(q).start()

    each(NQ, prepare_and_send)
    double(p)
    def pass_on(n):
        i = 15 - n

        def body():
            ag(i).wait_recv()
            hand_on(i, core).start()

        guard(i, core, body)

    each(16, pass_on)

    def settle(q):
        w_copy(q).wait_recv()

    each(NQ, settle)
    wide = lax.broadcasted_iota(I32, (48, 128), 1)

    def assemble(f):
        rows = pl.ds(pl.multiple_of(48 * f, 48), 48)
        tiles = [wown[q, rows, :] + wrecv[q, rows, :] for q in range(NQ)]
        for c in range(5):
            value = None
            for q in range(NQ):
                begin, end = KQ * q - 128 * c, KQ * (q + 1) - 128 * c
                if end <= 0 or begin >= 128:
                    continue
                value = tiles[q] if value is None else jnp.where(wide < begin, value, tiles[q])
            lhs[rows, 128 * c : 128 * c + 128] = value.astype(BF16)

    each(NB, assemble)
    def double_own(n):
        for u in range(4):
            double(slot(pick(4 * n + u, core), -1))

    each(4, double_own)

    def receive(n):
        for u in range(4):
            i = 15 - 4 * n - u
            guard(i, other, hand_on(i, other).wait_recv)
        for u in range(4):
            double(slot(pick(15 - 4 * n - u, other), -1))

    each(4, receive)
    c_mom.wait()
    c_tab.wait()

    def build(step):
        ref = rhs[step % 2]
        for part in range(4):
            x = 2 * (16 * core + plane(ORDER[4 * step + part], 1))
            for q in range(NQ):
                shift = momv[q, 0]
                qx = shift // 64
                amount = (128 - shift % 64) % 128
                first = pltpu.roll(dup[(x + qx) % 64], amount, 1)
                second = pltpu.roll(dup[(x + 1 + qx) % 64], amount, 1)
                ref[KQ * q : KQ * q + 80, 128 * part : 128 * part + 128] = jnp.where(low, first, second)

    def encode(flow, ref):
        top = jnp.abs(flow[0:8])
        for t in range(1, 6):
            top = jnp.maximum(top, jnp.abs(flow[8 * t : 8 * t + 8]))
        power = jnp.floor(jnp.log2(jnp.maximum(top, 2.0**-100))) + 1.0
        unit = jnp.exp2(BITS - power)
        parts = [jnp.round(flow[8 * t : 8 * t + 8] * unit) for t in range(6)]
        ref[...] = jnp.concatenate(parts + [power, power], axis=0).astype(I32).astype(jnp.int16)

    def decode(ref):
        values = ref[...].astype(I32).astype(F32)
        unit = jnp.exp2(values[48:56] - BITS)
        return jnp.concatenate([values[8 * t : 8 * t + 8] * unit for t in range(6)], axis=0)

    def s_copy(e):
        return remote(ssend.at[e], srecv.at[e], s_s.at[e], s_r.at[e], (zl * 16 + plane(e, 1), wa))

    def contract(step):
        acc = jnp.dot(lhs[...], rhs[step % 2][...], preferred_element_type=F32)
        for part in range(4):
            e = ORDER[4 * step + part]
            factors = tab[plane(e, 1)]
            flow = None
            for f in range(NB):
                term = factors[f : f + 1, :] * acc[48 * f : 48 * f + 48, 128 * part : 128 * part + 128]
                flow = term if flow is None else flow + term
            if e:
                encode(flow, ssend.at[e])
            else:
                red[0:48, :] = flow
        for part in range(4):
            if ORDER[4 * step + part]:
                s_copy(ORDER[4 * step + part]).start()

    rhs = (rhs0, rhs1)
    build(0)
    for step in range(4):
        if step < 3:
            build(step + 1)
        contract(step)

    for group in (ORDER[0:11], ORDER[11:15]):
        for e in group:
            s_copy(e).wait_recv()
        flow = red[0:48, :]
        for e in group:
            flow = flow + decode(srecv.at[e])
        red[0:48, :] = flow

    def f_copy(d):
        owner = 2 * ((wa // 2 + d // 2) % 4) + (core + d) % 2
        return remote(fsend.at[owner], frecv.at[z], f_s.at[d], f_r.at[z], (core * 16 + p % 16, owner))

    def f_arrival(d):
        k = (z + d) % 8
        return remote(fsend.at[0], frecv.at[k], f_s.at[0], f_r.at[k], ((k % 2) * 16 + p % 16, (k // 2) * 2 + zl))

    for j in range(8):
        fsend[j, 0:6, :] = red[6 * j : 6 * j + 6, :]
    for d in (4, 5, 2, 3, 6, 7, 1):
        f_copy(d).start()

    @pl.when(core != zl)
    def _():
        f_copy(0).start()
        f_arrival(0).wait_recv()

    @pl.when(core == zl)
    def _():
        frecv[z] = fsend[wa]

    def drain(i):
        def body():
            ag(i).wait_send()
            hand_on(i, core).wait_send()

        guard(i, core, body)

    each(16, drain)
    each(NQ, lambda q: w_copy(q).wait_send())
    each(15, lambda i: s_copy(i + 1).wait_send())

    for d in range(1, 8):
        f_copy(d).wait_send()

    @pl.when(core != zl)
    def _():
        f_copy(0).wait_send()

    for d in (1, 7, 2, 6, 3, 5, 4):
        f_arrival(d).wait_recv()
    total = frecv[0]
    for k in range(1, 8):
        total = total + frecv[k]
    out[...] = total[0:6]


def local(propagator, vertex, momentum_shift, frequency_shift):
    rows = vertex.transpose(0, 2, 1).reshape(3600, 128, 2).transpose(0, 2, 1).reshape(7200, 128)
    dma = pltpu.SemaphoreType.DMA
    vmem = pltpu.VMEM
    scratch = [
        vmem((7200, 128), BF16),
        vmem((7264, 128), F32),
        vmem((NQ, ROWS + 16, 128), F32),
        vmem((NQ, ROWS, 128), F32),
        vmem((ROWS, NQ * KQ), BF16),
        vmem((32, 80, 128), BF16),
        vmem((64, 80, 128), BF16),
        vmem((NQ * KQ, 512), BF16),
        vmem((NQ * KQ, 512), BF16),
        vmem((16, 16, 128), F32),
        pltpu.SMEM((8, 128), I32),
        pltpu.SMEM((2, 48), I32),
        vmem((16, 64, 128), jnp.int16),
        vmem((16, 64, 128), jnp.int16),
        vmem((56, 128), F32),
        vmem((8, 8, 128), F32),
        vmem((8, 8, 128), F32),
        dma((4,)),
        dma((9,)),
    ]
    scratch += [dma((8,))] * 4 + [dma((16,))] * 6
    return pl.pallas_call(
        kernel,
        out_shape=jax.ShapeDtypeStruct((6, 128), F32),
        in_specs=[pl.BlockSpec(memory_space=pltpu.HBM)] * 5,
        out_specs=pl.BlockSpec(memory_space=pltpu.VMEM),
        scratch_shapes=scratch,
        compiler_params=pltpu.CompilerParams(
            collective_id=0, has_side_effects=True, vmem_limit_bytes=56549376
        ),
    )(propagator, rows, momentum_shift, frequency_shift, jnp.asarray(minus_functions()))


def solution(mesh):
    from jax.sharding import PartitionSpec as P

    in_specs = (P(None, "pb"), P("pb", "wa", None), P("pb", None), P("wa", None))
    out_specs = P("wa", "pb")
    return jax.shard_map(local, mesh=mesh, in_specs=in_specs, out_specs=out_specs, check_vma=False)
```

```python
import math

import jax
import jax.numpy as jnp
import numpy as np
from jax import lax
from jax.experimental import pallas as pl
from jax.experimental.pallas import tpu as pltpu

LAT = 64
F32 = jnp.float32
BF16 = jnp.bfloat16
I32 = jnp.int32
NQ = 8
NB = 13
ROWS = NB * 48
KQ = 80
BITS = 14.0
ORDER = (10, 9, 11, 14, 6, 8, 2, 13, 7, 5, 15, 4, 12, 1, 3, 0)

BLOCKS = (
    ((0, 0, 1), (1, 1, 1), (2, 2, 1), (3, 3, 1), (4, 4, 1)),
    ((0, 1, 1), (1, 0, 1)),
    ((0, 2, 1), (2, 0, 1)),
    ((0, 3, 1), (3, 0, 1)),
    ((0, 4, 1), (4, 0, 1)),
    ((1, 1, 1), (3, 3, -1)),
    ((1, 3, 1), (3, 1, 1)),
    ((2, 2, 1), (4, 4, -1)),
    ((2, 4, 1), (4, 2, 1)),
    ((1, 2, 1), (2, 1, 1)),
    ((1, 4, 1), (4, 1, 1)),
    ((2, 3, 1), (3, 2, 1)),
    ((3, 4, 1), (4, 3, 1)),
)


def minus_functions():
    k = np.arange(LAT * LAT)
    a = (k // LAT) * (2.0 * math.pi / LAT)
    b = (k % LAT) * (2.0 * math.pi / LAT)
    root = math.sqrt(2.0)
    ca, cb, sa, sb = np.cos(a), np.cos(b), np.sin(a), np.sin(b)
    rows = [
        np.ones_like(a),
        root * ca,
        root * cb,
        root * sa,
        root * sb,
        np.cos(2 * a),
        np.sin(2 * a),
        np.cos(2 * b),
        np.sin(2 * b),
        2 * ca * cb,
        2 * ca * sb,
        2 * cb * sa,
        2 * sa * sb,
    ]
    table = np.zeros((16, LAT * LAT), np.float32)
    table[:NB] = -np.stack(rows)
    return np.ascontiguousarray(table.reshape(16, 32, 128).transpose(1, 0, 2))


def kernel(
    prop, vert, mom, freq, table, out,
    vb, s32, wown, wrecv, lhs, gs, dup, rhs0, rhs1, tab, momv, freqv,
    ssend, srecv, red, fsend, frecv,
    in_sem, v_sem, w_s, w_r, f_s, f_r, ag_s, ag_r, c_s, c_r, s_s, s_r,
):
    p = lax.axis_index("pb")
    wa = lax.axis_index("wa")
    zl = p // 16
    yy = (p // 4) % 4
    xx = p % 4
    core = wa % 2
    z = (wa // 2) * 2 + zl
    other = 1 - core
    sibling = (p, (wa // 2) * 2 + other)

    def remote(src, dst, send, recv, device):
        return pltpu.make_async_remote_copy(
            src_ref=src, dst_ref=dst, send_sem=send, recv_sem=recv,
            device_id=device, device_id_type=pl.DeviceIdType.MESH,
        )

    def signal(device):
        pl.semaphore_signal(barrier, inc=1, device_id=device, device_id_type=pl.DeviceIdType.MESH)

    def each(n, body):
        def step(i, carry):
            body(i)
            return carry

        lax.fori_loop(0, n, step, 0)

    def pick(i, which):
        y = (i // 4 + 2) % 4
        x = (i % 4 + 2) % 4
        return ((which + y + x) % 2, y, x)

    def slot(o, sign):
        a, y, x = o
        return ((zl + a) % 2) * 16 + ((yy + sign * y + 4) % 4) * 4 + (xx + sign * x + 4) % 4

    def plane(e, sign):
        return ((yy + sign * (e // 4) + 4) % 4) * 4 + (xx + sign * (e % 4) + 4) % 4

    def mate(o):
        zz = (z + o[0] * (1 - 2 * zl) + 8) % 8
        return (slot(o, 1), (zz // 2) * 2 + core)

    barrier = pltpu.get_barrier_semaphore()
    def guard(i, which, body):
        pl.when((i != 10) | (which == 1))(body)

    each(16, lambda i: guard(i, core, lambda: signal(mate(pick(i, core)))))

    def greet_along(d):
        zz = (z + 1 + d) % 8
        signal(((zz % 2) * 16 + p % 16, (zz // 2) * 2 + zl))

    def greet_plane(i):
        y = (i // 2 + 2) % 4
        x = 2 * (i % 2) + (y + core + 1) % 2

        @pl.when(4 * y + x != 0)
        def _():
            signal(mate((0, y, x)))

    each(7, greet_along)
    each(8, greet_plane)

    @pl.when(core != zl)
    def _():
        signal(sibling)

    signal(sibling)

    c_mom = pltpu.make_async_copy(mom.at[:, pl.ds(0, 128)], momv, in_sem.at[0])
    c_freq = pltpu.make_async_copy(freq, freqv, in_sem.at[1])
    c_tab = pltpu.make_async_copy(table.at[pl.ds(core * 16, 16)], tab, in_sem.at[2])
    c_own = pltpu.make_async_copy(prop, gs.at[p], in_sem.at[3])
    c_freq.start()

    def piece(i):
        rows = pl.ds(pl.multiple_of(i * 800, 800), 800)
        return pltpu.make_async_copy(vert.at[rows], vb.at[rows], v_sem.at[i])

    each(9, lambda i: piece(i).start())
    c_mom.start()
    c_own.start()
    c_tab.start()

    def widen(i):
        piece(i).wait()
        for t in range(5):
            rows = pl.ds(pl.multiple_of(i * 800 + t * 160, 160), 160)
            s32[rows, :] = vb[rows, :].astype(F32)

    each(9, widen)
    s32[pl.ds(7200, 64), :] = jnp.zeros((64, 128), F32)

    lane = lax.broadcasted_iota(I32, (8, 128), 1)
    c_freq.wait()

    def prepare(q):
        place = [(KQ * q) % 128 + freqv[w, 0] for w in range(2)]
        valid = [(lane + 256 - o) % 128 < 48 for o in place]
        for i in range(8):
            total = [None] * NB
            for w in range(2):
                blocks = {}
                for n2 in range(5):
                    off = 240 * i + 48 * n2
                    s, start = off // 128, off % 128
                    amount = (place[w] + (128 - start)) % 128
                    for n in range(5):
                        row = q * 900 + 180 * n + w + 2 * s
                        value = s32[pl.ds(row, 8, stride=30), :]
                        if start > 80:
                            after = s32[pl.ds(row + 2, 8, stride=30), :]
                            value = jnp.where(lane < start, after, value)
                        blocks[n, n2] = pltpu.roll(value, amount, 1)
                for f in range(NB):
                    term = None
                    for n, n2, sign in BLOCKS[f]:
                        if term is None:
                            term = blocks[n, n2]
                        elif sign > 0:
                            term = term + blocks[n, n2]
                        else:
                            term = term - blocks[n, n2]
                    term = jnp.where(valid[w], term, 0.0)
                    total[f] = term if total[f] is None else total[f] + term
            for f in range(NB):
                wown[q, pl.ds(48 * f + i, 6, stride=8), :] = total[f][0:6]

    c_own.wait()
    pl.semaphore_wait(barrier, 31 + core + zl - 2 * core * zl)

    def ag(i):
        return remote(gs.at[p], gs.at[p], ag_s.at[i], ag_r.at[i], mate(pick(i, core)))

    def w_copy(q):
        return remote(wown.at[q, pl.ds(0, ROWS)], wrecv.at[q], w_s.at[q], w_r.at[q], sibling)

    def hand_on(i, which):
        block = slot(pick(i, which), -1)
        return remote(gs.at[block], gs.at[block], c_s.at[i], c_r.at[i], sibling)

    low = lax.broadcasted_iota(I32, (80, 128), 1) < 64

    def double(b):
        value = gs[b]
        turned = pltpu.roll(value, 64, 1)
        dup[2 * b] = jnp.where(low, value, turned)
        dup[2 * b + 1] = jnp.where(low, turned, value)

    each(16, lambda i: guard(i, core, lambda: ag(i).start()))

    def prepare_and_send(q):
        prepare(q)
        w_copy(q).start()

    each(NQ, prepare_and_send)
    double(p)
    def pass_on(n):
        i = 15 - n

        def body():
            ag(i).wait_recv()
            hand_on(i, core).start()

        guard(i, core, body)

    each(8, pass_on)

    def settle(q):
        w_copy(q).wait_recv()

    each(NQ, settle)
    wide = lax.broadcasted_iota(I32, (48, 128), 1)

    def assemble(f):
        rows = pl.ds(pl.multiple_of(48 * f, 48), 48)
        tiles = [wown[q, rows, :] + wrecv[q, rows, :] for q in range(NQ)]
        for c in range(5):
            value = None
            for q in range(NQ):
                begin, end = KQ * q - 128 * c, KQ * (q + 1) - 128 * c
                if end <= 0 or begin >= 128:
                    continue
                value = tiles[q] if value is None else jnp.where(wide < begin, value, tiles[q])
            lhs[rows, 128 * c : 128 * c + 128] = value.astype(BF16)

    def double_own(n):
        for u in range(4):
            double(slot(pick(4 * n + u, core), -1))

    each(NB, assemble)
    each(2, lambda n: double_own(n + 2))
    each(8, lambda n: pass_on(n + 8))
    each(2, double_own)

    def receive(n):
        for u in range(4):
            i = 15 - 4 * n - u
            guard(i, other, hand_on(i, other).wait_recv)
        for u in range(4):
            double(slot(pick(15 - 4 * n - u, other), -1))

    each(4, receive)
    c_mom.wait()
    c_tab.wait()

    def build(step):
        ref = rhs[step % 2]
        for part in range(4):
            x = 2 * (16 * core + plane(ORDER[4 * step + part], 1))
            for q in range(NQ):
                shift = momv[q, 0]
                qx = shift // 64
                amount = (128 - shift % 64) % 128
                first = pltpu.roll(dup[(x + qx) % 64], amount, 1)
                second = pltpu.roll(dup[(x + 1 + qx) % 64], amount, 1)
                ref[KQ * q : KQ * q + 80, 128 * part : 128 * part + 128] = jnp.where(low, first, second)

    def encode(flow, ref):
        top = jnp.abs(flow[0:8])
        for t in range(1, 6):
            top = jnp.maximum(top, jnp.abs(flow[8 * t : 8 * t + 8]))
        power = jnp.floor(jnp.log2(jnp.maximum(top, 2.0**-100))) + 1.0
        unit = jnp.exp2(BITS - power)
        parts = [jnp.round(flow[8 * t : 8 * t + 8] * unit) for t in range(6)]
        ref[...] = jnp.concatenate(parts + [power, power], axis=0).astype(I32).astype(jnp.int16)

    def decode(ref):
        values = ref[...].astype(I32).astype(F32)
        unit = jnp.exp2(values[48:56] - BITS)
        return jnp.concatenate([values[8 * t : 8 * t + 8] * unit for t in range(6)], axis=0)

    def s_copy(e):
        return remote(ssend.at[e], srecv.at[e], s_s.at[e], s_r.at[e], (zl * 16 + plane(e, 1), wa))

    def contract(step):
        acc = jnp.dot(lhs[...], rhs[step % 2][...], preferred_element_type=F32)
        for part in range(4):
            e = ORDER[4 * step + part]
            factors = tab[plane(e, 1)]
            flow = None
            for f in range(NB):
                term = factors[f : f + 1, :] * acc[48 * f : 48 * f + 48, 128 * part : 128 * part + 128]
                flow = term if flow is None else flow + term
            if e:
                encode(flow, ssend.at[e])
            else:
                red[0:48, :] = flow
        for part in range(4):
            if ORDER[4 * step + part]:
                s_copy(ORDER[4 * step + part]).start()

    rhs = (rhs0, rhs1)
    build(0)
    for step in range(4):
        if step < 3:
            build(step + 1)
        contract(step)

    for group in (ORDER[0:11], ORDER[11:15]):
        for e in group:
            s_copy(e).wait_recv()
        flow = red[0:48, :]
        for e in group:
            flow = flow + decode(srecv.at[e])
        red[0:48, :] = flow

    def f_copy(d):
        owner = 2 * ((wa // 2 + d // 2) % 4) + (core + d) % 2
        return remote(fsend.at[owner], frecv.at[z], f_s.at[d], f_r.at[z], (core * 16 + p % 16, owner))

    def f_arrival(d):
        k = (z + d) % 8
        return remote(fsend.at[0], frecv.at[k], f_s.at[0], f_r.at[k], ((k % 2) * 16 + p % 16, (k // 2) * 2 + zl))

    for j in range(8):
        fsend[j, 0:6, :] = red[6 * j : 6 * j + 6, :]
    for d in (4, 5, 2, 3, 6, 7, 1):
        f_copy(d).start()

    @pl.when(core != zl)
    def _():
        f_copy(0).start()
        f_arrival(0).wait_recv()

    @pl.when(core == zl)
    def _():
        frecv[z] = fsend[wa]

    def drain(i):
        def body():
            ag(i).wait_send()
            hand_on(i, core).wait_send()

        guard(i, core, body)

    each(16, drain)
    each(NQ, lambda q: w_copy(q).wait_send())
    each(15, lambda i: s_copy(i + 1).wait_send())

    for d in range(1, 8):
        f_copy(d).wait_send()

    @pl.when(core != zl)
    def _():
        f_copy(0).wait_send()

    for d in (1, 7, 2, 6, 3, 5, 4):
        f_arrival(d).wait_recv()
    total = frecv[0]
    for k in range(1, 8):
        total = total + frecv[k]
    out[...] = total[0:6]


def local(propagator, vertex, momentum_shift, frequency_shift):
    rows = vertex.transpose(0, 2, 1).reshape(3600, 128, 2).transpose(0, 2, 1).reshape(7200, 128)
    dma = pltpu.SemaphoreType.DMA
    vmem = pltpu.VMEM
    scratch = [
        vmem((7200, 128), BF16),
        vmem((7264, 128), F32),
        vmem((NQ, ROWS + 16, 128), F32),
        vmem((NQ, ROWS, 128), F32),
        vmem((ROWS, NQ * KQ), BF16),
        vmem((32, 80, 128), BF16),
        vmem((64, 80, 128), BF16),
        vmem((NQ * KQ, 512), BF16),
        vmem((NQ * KQ, 512), BF16),
        vmem((16, 16, 128), F32),
        pltpu.SMEM((8, 128), I32),
        pltpu.SMEM((2, 48), I32),
        vmem((16, 64, 128), jnp.int16),
        vmem((16, 64, 128), jnp.int16),
        vmem((56, 128), F32),
        vmem((8, 8, 128), F32),
        vmem((8, 8, 128), F32),
        dma((4,)),
        dma((9,)),
    ]
    scratch += [dma((8,))] * 4 + [dma((16,))] * 6
    return pl.pallas_call(
        kernel,
        out_shape=jax.ShapeDtypeStruct((6, 128), F32),
        in_specs=[pl.BlockSpec(memory_space=pltpu.HBM)] * 5,
        out_specs=pl.BlockSpec(memory_space=pltpu.VMEM),
        scratch_shapes=scratch,
        compiler_params=pltpu.CompilerParams(
            collective_id=0, has_side_effects=True, vmem_limit_bytes=56549376
        ),
    )(propagator, rows, momentum_shift, frequency_shift, jnp.asarray(minus_functions()))


def solution(mesh):
    from jax.sharding import PartitionSpec as P

    in_specs = (P(None, "pb"), P("pb", "wa", None), P("pb", None), P("wa", None))
    out_specs = P("wa", "pb")
    return jax.shard_map(local, mesh=mesh, in_specs=in_specs, out_specs=out_specs, check_vma=False)
```
